32 devices in a mesh: dp: 2 (over y), space: 16 (over z, x, core).
Axes of the slice: x: 2, y: 2, z: 4, core: 2. Of those that a mesh axis runs over, the one named last changes fastest.
Arguments:
- fields: bfloat16 [2, 128, 128, 512], P('dp', 'space'), may hold values from -6 to 6
- bn_scale: float32 [512], replicated, may hold values from 0.5 to 1.5
- bn_shift: float32 [512], replicated, may hold values from -3 to 3
- w_expand: bfloat16 [512, 2048], P(None, 'dp'), may hold values from -0.25 to 0.25
- expand_bias: float32 [2048], replicated, may hold values from -3 to 3
- dw_kernel: float32 [3, 3, 2048], replicated, may hold values from -2 to 2
- dw_bias: float32 [2048], replicated, may hold values from -3 to 3
- w_project: bfloat16 [2048, 512], P(None, 'dp'), may hold values from -0.125 to 0.125
- ln_gain: float32 [512], replicated, may hold values from 0.5 to 1.5
- ln_bias: float32 [512], replicated, may hold values from -3 to 3
- w_qkv: bfloat16 [512, 1536], P(None, 'dp'), may hold values from -0.25 to 0.25
- w_out: bfloat16 [512, 512], P(None, 'dp'), may hold values from -0.25 to 0.25
Outputs:
- output: bfloat16 [2, 128, 128, 512], P('dp', 'space')
The draws below stay inside these ranges and needn't reach their ends.
All inputs are finite; a program needn't handle non-finite values.
Results may differ from the reference program's by a relative error of at most 0.0056.
Values may be sent and summed in bfloat16 or wider, within the bound.
No kernel may reach another device: no remote copies, remote signals or barrier semaphores. Data moves between devices by JAX's collectives and lax.ppermute only.
A program may use at most 64 MiB of HBM per device.

```python
import jax
import jax.numpy as jnp
from jax import lax

C = 512
FF = 2048
HD = 32
GRID = 8
HEIGHT = 128
COLS = 128
SAMPLES = 2


def block_levels(own_key, extent, shards, low, largest):
    factor_of, own = 1.0, jax.random.fold_in(own_key, 6)
    for axis_at, shards_of in shards:
        draws = jnp.exp(jax.random.uniform(jax.random.fold_in(own, axis_at), (shards_of,), jnp.float32, low / len(shards), largest / len(shards)))
        factor_of = factor_of * jnp.repeat(draws, extent[axis_at] // shards_of).reshape([-1 if axis == axis_at else 1 for axis in range(len(extent))])
    return factor_of


def normal_values(rng, shape, scale, reach, shards=(), dtype=jnp.bfloat16):
    array = jax.random.normal(rng, shape, jnp.float32) * scale
    if len(shards) > 0:
        array = block_levels(rng, shape, shards, -0.22, 0.18) * array
    return jnp.clip(array, min=-reach, max=reach).astype(dtype)


def setup_inputs(seed: int = 0) -> dict:
    arg_keys = jax.random.split(jax.random.key(seed), 13)
    return {
        "fields": normal_values(arg_keys[0], (SAMPLES, HEIGHT, COLS, C), 1.0, 6.0, ((0, 2), (1, 16))),
        "bn_scale": jnp.clip(1.0 + 0.1 * jax.random.normal(arg_keys[1], (C,), jnp.float32), 0.5, 1.5),
        "bn_shift": normal_values(arg_keys[2], (C,), 0.5, 3.0, (), jnp.float32),
        "w_expand": normal_values(arg_keys[3], (C, FF), C ** -0.5, 0.25, ((1, 2),)),
        "expand_bias": normal_values(arg_keys[4], (FF,), 0.5, 3.0, (), jnp.float32),
        "dw_kernel": normal_values(arg_keys[5], (3, 3, FF), 9 ** -0.5, 2.0, (), jnp.float32),
        "dw_bias": normal_values(arg_keys[6], (FF,), 0.5, 3.0, (), jnp.float32),
        "w_project": normal_values(arg_keys[7], (FF, C), FF ** -0.5, 0.125, ((1, 2),)),
        "ln_gain": jnp.clip(1.0 + 0.1 * jax.random.normal(arg_keys[8], (C,), jnp.float32), 0.5, 1.5),
        "ln_bias": normal_values(arg_keys[9], (C,), 0.4, 3.0, (), jnp.float32),
        "w_qkv": normal_values(arg_keys[10], (C, 3 * C), C ** -0.5, 0.25, ((1, 2),)),
        "w_out": normal_values(arg_keys[11], (C, C), C ** -0.5, 0.25, ((1, 2),)),
    }


def layer_normed(tokens, ln_gain, ln_bias):
    values = tokens.astype(jnp.float32)
    center = lax.optimization_barrier(jnp.mean(values, axis=-1, keepdims=True))
    spread = lax.optimization_barrier(jnp.mean(jnp.square(values - center), axis=-1, keepdims=True))
    return ((values - center) * lax.rsqrt(spread + 1e-05) * ln_gain + ln_bias).astype(jnp.bfloat16)

def attend_windows(queries, keyset, valueset):
    window_count, length, width = queries.shape
    heads = width // HD
    query_heads = queries.reshape(window_count, length, heads, HD).astype(jnp.float32)
    key_heads = keyset.reshape(window_count, length, heads, HD).astype(jnp.float32)
    value_heads = valueset.reshape(window_count, length, heads, HD).astype(jnp.float32)
    scores = jnp.einsum('wqhd,wkhd->whqk', query_heads, key_heads) / jnp.sqrt(jnp.float32(HD))
    exponent = jnp.exp(scores)
    soft_weights = (exponent / lax.optimization_barrier(jnp.sum(exponent, axis=-1, keepdims=True))).astype(jnp.bfloat16)
    mixed = jnp.einsum('whqk,wkhd->wqhd', soft_weights.astype(jnp.float32), value_heads)
    return mixed.astype(jnp.bfloat16).reshape(window_count, length, width)

def reference(fields, bn_scale, bn_shift, w_expand, expand_bias, dw_kernel, dw_bias, w_project, ln_gain, ln_bias, w_qkv, w_out):
    stride_rows = HEIGHT // GRID
    stride_cols = COLS // GRID

    def one_sample(sample):
        normed = (sample.astype(jnp.float32) * bn_scale + bn_shift).astype(jnp.bfloat16)
        expanded = jax.nn.gelu(jnp.dot(normed.reshape(-1, C), w_expand, preferred_element_type=jnp.float32) + expand_bias)
        expanded = expanded.astype(jnp.bfloat16).reshape(HEIGHT, COLS, FF)
        padded = jnp.pad(expanded, ((1, 1), (1, 1), (0, 0)))
        accum = jnp.zeros((HEIGHT, COLS, FF), jnp.float32)
        for row_off in range(3):
            for col_off in range(3):
                accum = accum + padded[row_off:row_off + HEIGHT, col_off:col_off + COLS].astype(jnp.float32) * dw_kernel[row_off, col_off]
        spatial = jax.nn.gelu(accum + dw_bias).astype(jnp.bfloat16)
        projected = jnp.dot(spatial.reshape(-1, FF), w_project, preferred_element_type=jnp.float32)
        conv_out = (sample.astype(jnp.float32) + projected.reshape(HEIGHT, COLS, C)).astype(jnp.bfloat16)
        normal_two = layer_normed(conv_out, ln_gain, ln_bias)
        triple = jnp.dot(normal_two.reshape(-1, C), w_qkv, preferred_element_type=jnp.float32).astype(jnp.bfloat16)
        grouped = triple.reshape(GRID, stride_rows, GRID, stride_cols, 3 * C).transpose(1, 3, 0, 2, 4)
        grouped = grouped.reshape(stride_rows * stride_cols, GRID * GRID, 3 * C)
        attended = attend_windows(grouped[..., :C], grouped[..., C:2 * C], grouped[..., 2 * C:])
        restored = attended.reshape(stride_rows, stride_cols, GRID, GRID, C).transpose(2, 0, 3, 1, 4).reshape(HEIGHT * COLS, C)
        final = conv_out.astype(jnp.float32) + jnp.dot(restored, w_out, preferred_element_type=jnp.float32).reshape(HEIGHT, COLS, C)
        return final.astype(jnp.bfloat16)
    return lax.map(one_sample, fields)
```

```python
import functools
import math

import jax
import jax.numpy as jnp
from jax import lax
from jax.experimental import pallas as pl
from jax.experimental.pallas import tpu as pltpu
from jax.sharding import PartitionSpec as P

HD = 32
GRID = 8
CHUNKS = 2
ROOT = math.sqrt(2.0 / math.pi)
LIN = 2.0 * ROOT
CUBE = 8.0 * ROOT * 0.044715
F32 = jnp.float32
BF16 = jnp.bfloat16
VMEM_LIMIT = 56 * 1024 * 1024


def half_gelu(half):
    return half + half * jnp.tanh(half * (LIN + CUBE * (half * half)))


def one_hot_order(cols, inverse=False):
    stride = cols // GRID
    row = lax.broadcasted_iota(jnp.int32, (cols, cols), 0)
    col = lax.broadcasted_iota(jnp.int32, (cols, cols), 1)
    if inverse:
        row, col = col, row
    return jnp.where(col == (row % GRID) * stride + row // GRID, 1.0, 0.0).astype(BF16)


def dot(a, b):
    return jnp.dot(a, b, preferred_element_type=F32)


def vmem():
    return pl.BlockSpec(memory_space=pltpu.VMEM)


def smem():
    return pl.BlockSpec(memory_space=pltpu.SMEM)


def params():
    return pltpu.CompilerParams(vmem_limit_bytes=VMEM_LIMIT)


def order_kernel(fields, scale, shift, ordered, normed):
    rows, cols, _ = fields.shape
    pick = one_hot_order(cols)
    for row in range(rows):
        placed = dot(pick, fields[row])
        ordered[row] = placed.astype(BF16)
        normed[row] = (placed * (0.5 * scale[...]) + 0.5 * shift[...]).astype(BF16)


def order_rows(fields, scale, shift):
    shape = jax.ShapeDtypeStruct(fields.shape, BF16)
    return pl.pallas_call(
        order_kernel,
        out_shape=(shape, shape),
        in_specs=[vmem()] * 3,
        out_specs=(vmem(), vmem()),
        compiler_params=params(),
        name="order_rows",
    )(fields, scale, shift)


def expand_kernel(pieces, aliased, info, normed, above, below, scale, shift, *refs):
    weights = refs[:pieces]
    bias, taps, tap_bias = refs[pieces : pieces + 3]
    out, edge, wide = refs[pieces + 3 + aliased :]
    rows, cols, _ = normed.shape
    width = bias.shape[-1]

    @pl.when(pl.program_id(0) == 0)
    def _():
        pick = one_hot_order(cols)
        for side, ref in enumerate((above, below)):
            placed = dot(pick, ref[0])
            edge[side] = (placed * (0.5 * scale[...]) + 0.5 * shift[...]).astype(BF16)

    half_bias = 0.5 * bias[...]
    half_taps = 0.5 * taps[...]
    half_tap_bias = 0.5 * tap_bias[...]
    lane = lax.broadcasted_iota(jnp.int32, (GRID, width), 0)
    for row in range(rows + 2):
        total = half_bias
        for piece, weight in enumerate(weights):
            depth = weight.shape[0]
            if pieces == 1:
                span = slice(None)
            else:
                span = pl.ds(pl.multiple_of(info[3 + piece] * depth, depth), depth)
            if row == 0:
                tokens = edge[0, :, span]
            elif row == rows + 1:
                tokens = edge[1, :, span]
            else:
                tokens = normed[row - 1, :, span]
            total = total + dot(tokens, weight[...])
        value = half_gelu(total)
        if row == 0:
            value = value * info[1].astype(F32)
        elif row == rows + 1:
            value = value * info[2].astype(F32)
        wide[row, GRID : GRID + cols, :] = value
        first = value[:GRID]
        last = value[cols - GRID :]
        wide[row, :GRID, :] = jnp.where(lane == 0, 0.0, pltpu.roll(last, 1, 0))
        wide[row, GRID + cols :, :] = jnp.where(
            lane == GRID - 1, 0.0, pltpu.roll(first, GRID - 1, 0)
        )
        if row >= 2:
            total = half_tap_bias
            for row_off in range(3):
                for col_off in range(3):
                    total = (
                        total
                        + wide[row - 2 + row_off, GRID * col_off : GRID * col_off + cols, :]
                        * half_taps[row_off, col_off][None]
                    )
            out[(row - 2) * cols : (row - 1) * cols, :] = half_gelu(total).astype(BF16)


def expand_some(normed, above, below, scale, shift, weights, info, bias, taps, tap_bias, spatial):
    rows, cols, chans = normed.shape
    inner = bias.shape[-1]
    here = weights[0].shape[1]
    width = min(256, here)
    aliased = spatial is not None
    whole = lambda shape: pl.BlockSpec(shape, lambda t, info: (0,) * len(shape))
    in_specs = [
        whole(normed.shape),
        whole(above.shape),
        whole(below.shape),
        whole(scale.shape),
        whole(shift.shape),
    ]
    in_specs += [pl.BlockSpec((w.shape[0], width), lambda t, info: (0, t)) for w in weights]
    in_specs += [
        pl.BlockSpec((1, width), lambda t, info: (0, info[0] + t)),
        pl.BlockSpec((3, 3, width), lambda t, info: (0, 0, info[0] + t)),
        pl.BlockSpec((1, width), lambda t, info: (0, info[0] + t)),
    ]
    operands = [info, normed, above, below, scale, shift, *weights, bias, taps, tap_bias]
    aliases = {}
    if aliased:
        in_specs.append(pl.BlockSpec(memory_space=pl.ANY))
        aliases = {len(operands): 0}
        operands.append(spatial)
    return pl.pallas_call(
        functools.partial(expand_kernel, len(weights), int(aliased)),
        grid_spec=pltpu.PrefetchScalarGridSpec(
            num_scalar_prefetch=1,
            grid=(here // width,),
            in_specs=in_specs,
            out_specs=pl.BlockSpec((rows * cols, width), lambda t, info: (0, info[0] + t)),
            scratch_shapes=[
                pltpu.VMEM((2, cols, chans), BF16),
                pltpu.VMEM((rows + 2, cols + 2 * GRID, width), F32),
            ],
        ),
        out_shape=jax.ShapeDtypeStruct((rows * cols, inner), BF16),
        input_output_aliases=aliases,
        compiler_params=params(),
        name="expand_conv",
    )(*operands)


def assemble(target, pieces, info):
    for n, piece in enumerate(pieces):
        depth, width = piece.shape
        if piece.shape == target.shape:
            target[...] = piece[...]
        else:
            target[
                pl.ds(pl.multiple_of(info[2 * n] * depth, depth), depth),
                pl.ds(pl.multiple_of(info[2 * n + 1] * width, width), width),
            ] = piece[...]


def project_kernel(pieces, info, spatial, ordered, *refs):
    weights = refs[:pieces]
    outs = refs[pieces : pieces + GRID]
    full, conv = refs[pieces + GRID :]

    @pl.when(pl.program_id(0) == 0)
    def _():
        assemble(full, weights, [info[1 + n] for n in range(2 * pieces)])

    conv[...] = (ordered[0].astype(F32) + dot(spatial[...], full[...])).astype(BF16)
    size = outs[0].shape[1]
    for k in range(GRID):
        start = pl.multiple_of((info[0] ^ k) * size, size)
        outs[k][0] = conv[pl.ds(start, size), :]


def project_rows(spatial, ordered, weights, info, first, count):
    rows, cols, chans = ordered.shape
    inner = spatial.shape[1]
    size = cols // GRID
    out = jax.ShapeDtypeStruct((count, size, chans), BF16)
    whole = lambda shape: pl.BlockSpec(shape, lambda t, info: (0,) * len(shape))
    return pl.pallas_call(
        functools.partial(project_kernel, len(weights)),
        grid_spec=pltpu.PrefetchScalarGridSpec(
            num_scalar_prefetch=1,
            grid=(count,),
            in_specs=[
                pl.BlockSpec((cols, inner), lambda t, info: (first + t, 0)),
                pl.BlockSpec((1, cols, chans), lambda t, info: (first + t, 0, 0)),
            ]
            + [whole(w.shape) for w in weights],
            out_specs=[pl.BlockSpec((1, size, chans), lambda t, info: (t, 0, 0))] * GRID,
            scratch_shapes=[pltpu.VMEM((inner, chans), BF16), pltpu.VMEM((cols, chans), BF16)],
        ),
        out_shape=[out] * GRID,
        compiler_params=params(),
        name="project_rows",
    )(info, spatial, ordered, *weights)


def attend_kernel(n_qkv, n_out, info, gain, bias, *refs):
    refs = list(refs)
    take = lambda n: [refs.pop(0) for _ in range(n)]
    qkv_pieces, out_pieces = take(n_qkv), take(n_out)
    tokens, outs = take(GRID), take(GRID)
    qkv_full, out_full, lned, triple, mixed, resid = refs
    count, size, chans = tokens[0].shape
    wins = size // GRID
    length = GRID * GRID
    group = min(256, chans)
    heads = group // HD
    keys = heads * length

    assemble(qkv_full, qkv_pieces, [info[n] for n in range(2 * n_qkv)])
    assemble(out_full, out_pieces, [info[2 * n_qkv + n] for n in range(2 * n_out)])

    for a in range(count):
        rows = [tokens[k][a].astype(F32) for k in range(GRID)]
        for w in range(wins):
            x = jnp.concatenate([r[w * GRID : (w + 1) * GRID] for r in rows], axis=0)
            start = (a * wins + w) * length
            resid[start : start + length, :] = x
            center = jnp.mean(x, axis=-1, keepdims=True)
            off = x - center
            spread = jnp.mean(off * off, axis=-1, keepdims=True)
            lned[start : start + length, :] = (
                off * lax.rsqrt(spread + 1e-05) * gain[...] + bias[...]
            ).astype(BF16)

    triple[...] = dot(lned[...], qkv_full[...]).astype(BF16)

    def same(shape, row_block, col_block):
        row = lax.broadcasted_iota(jnp.int32, shape, 0) // row_block
        col = lax.broadcasted_iota(jnp.int32, shape, 1) // col_block
        return jnp.where(row == col, 1.0, 0.0).astype(BF16)

    spread_mask = same((keys, group), length, HD)
    sum_mask = same((256, 256), length, length)
    factor = math.log2(math.e) / math.sqrt(HD)
    for win in range(count * wins):
        at = slice(win * length, (win + 1) * length)
        for g in range(chans // group):
            cols = slice(g * group, (g + 1) * group)
            query = triple[at, cols]
            key = triple[at, chans + g * group : chans + (g + 1) * group]
            value = triple[at, 2 * chans + g * group : 2 * chans + (g + 1) * group]
            key_wide = jnp.concatenate([key] * heads, axis=0) * spread_mask
            value_wide = jnp.concatenate([value] * heads, axis=0) * spread_mask
            scores = lax.dot_general(
                query, key_wide, (((1,), (1,)), ((), ())), preferred_element_type=F32
            )
            exponent = jnp.minimum(jnp.exp2(scores * factor), 3.3895e38)
            rounded = exponent.astype(BF16)
            sums = jnp.concatenate(
                [dot(rounded[:, n : n + 256], sum_mask) for n in range(0, keys, 256)], axis=1
            )
            soft = (exponent / sums).astype(BF16)
            mixed[at, cols] = dot(soft, value_wide).astype(BF16)

    resid[...] = resid[...] + dot(mixed[...], out_full[...])
    for a in range(count):
        for k in range(GRID):
            parts = []
            for w in range(wins):
                start = (a * wins + w) * length + k * GRID
                parts.append(resid[start : start + GRID, :])
            outs[k][a] = jnp.concatenate(parts, axis=0).astype(BF16)


def attend(tokens, gain, bias, w_qkv, w_out, info):
    count, size, chans = tokens[0].shape
    total = count * size * GRID
    out = jax.ShapeDtypeStruct(tokens[0].shape, BF16)
    return pl.pallas_call(
        functools.partial(attend_kernel, len(w_qkv), len(w_out)),
        out_shape=[out] * GRID,
        in_specs=[smem()] + [vmem()] * (2 + len(w_qkv) + len(w_out) + GRID),
        out_specs=[vmem()] * GRID,
        scratch_shapes=[
            pltpu.VMEM((chans, 3 * chans), BF16),
            pltpu.VMEM((chans, chans), BF16),
            pltpu.VMEM((total, chans), BF16),
            pltpu.VMEM((total, 3 * chans), BF16),
            pltpu.VMEM((total, chans), BF16),
            pltpu.VMEM((total, chans), F32),
        ],
        compiler_params=params(),
        name="attend",
    )(info, gain, bias, *w_qkv, *w_out, *tokens)


def restore_kernel(aliased, info, *refs):
    parts = refs[:GRID]
    out, row_buf = refs[GRID + aliased :]
    _, cols, _ = out.shape
    size = parts[0].shape[1]
    for k in range(GRID):
        row_buf[pl.ds(pl.multiple_of((info[0] ^ k) * size, size), size), :] = parts[k][0]
    out[0] = dot(one_hot_order(cols, inverse=True), row_buf[...]).astype(BF16)


def restore_rows(parts, info, rows, first, out):
    count, size, chans = parts[0].shape
    cols = size * GRID
    aliased = out is not None
    in_specs = [pl.BlockSpec((1, size, chans), lambda t, info: (t, 0, 0))] * GRID
    operands = [info, *parts]
    aliases = {}
    if aliased:
        in_specs.append(pl.BlockSpec(memory_space=pl.ANY))
        aliases = {len(operands): 0}
        operands.append(out)
    return pl.pallas_call(
        functools.partial(restore_kernel, int(aliased)),
        grid_spec=pltpu.PrefetchScalarGridSpec(
            num_scalar_prefetch=1,
            grid=(count,),
            in_specs=in_specs,
            out_specs=pl.BlockSpec((1, cols, chans), lambda t, info: (first + t, 0, 0)),
            scratch_shapes=[pltpu.VMEM((cols, chans), BF16)],
        ),
        out_shape=jax.ShapeDtypeStruct((rows, cols, chans), BF16),
        input_output_aliases=aliases,
        compiler_params=params(),
        name="restore_rows",
    )(*operands)


def scalars(*values):
    return jnp.stack([jnp.asarray(v, jnp.int32) for v in values])


def local(
    fields,
    bn_scale,
    bn_shift,
    w_expand,
    expand_bias,
    dw_kernel,
    dw_bias,
    w_project,
    ln_gain,
    ln_bias,
    w_qkv,
    w_out,
):
    _, rows, cols, chans = fields.shape
    inner = expand_bias.shape[0]
    dp, space = lax.axis_size("dp"), lax.axis_size("space")
    dp_at, space_at = lax.axis_index("dp"), lax.axis_index("space")
    groups = space // GRID
    grid_at = space_at // groups
    pairs = dp == 2 and space % 2 == 0
    core = space_at % 2
    as_row = lambda v: v.reshape(1, -1)
    scale, shift = as_row(bn_scale), as_row(bn_shift)
    image = fields.reshape(rows, cols, chans)

    down = [(i, i + 1) for i in range(space - 1)]
    up = [(i + 1, i) for i in range(space - 1)]
    above = lax.ppermute(image[rows - 1 :], "space", down)
    below = lax.ppermute(image[:1], "space", up)

    def fetch(weight):
        if not pairs:
            return [lax.all_gather(weight, "dp", axis=1, tiled=True)], [0, 0]
        part = weight.shape[0] // 2
        mine = lax.dynamic_slice_in_dim(weight, core * part, part, axis=0)
        got = lax.ppermute(mine, "dp", [(0, 1), (1, 0)])
        other = lax.ppermute(got, "space", [(i, i ^ 1) for i in range(space)])
        return [weight, got, other], [0, dp_at, core, 1 - dp_at, 1 - core, 1 - dp_at]

    expand_all, _ = fetch(w_expand)
    project_all, project_at = fetch(w_project)
    qkv_all, qkv_at = fetch(w_qkv)
    out_all, out_at = fetch(w_out)

    ordered, normed = order_rows(image, scale, shift)
    top = (space_at > 0).astype(jnp.int32)
    bottom = (space_at < space - 1).astype(jnp.int32)
    some = functools.partial(expand_some, normed, above, below, scale, shift)
    small = (as_row(expand_bias), dw_kernel, as_row(dw_bias))
    if pairs:
        tiles = w_expand.shape[1] // min(256, w_expand.shape[1])
        info = scalars(dp_at * tiles, top, bottom, 0, 0)
        spatial = some([w_expand], info, *small, None)
        info = scalars((1 - dp_at) * tiles, top, bottom, core, 1 - core)
        spatial = some(expand_all[1:], info, *small, spatial)
    else:
        spatial = some(expand_all, scalars(0, top, bottom, 0, 0), *small, None)

    count = rows // CHUNKS
    swaps = [
        [(s, (((s // groups) ^ k) * groups) + s % groups) for s in range(space)]
        for k in range(GRID)
    ]
    order = (4, 6, 5, 7, 2, 3, 1)

    def exchange(parts):
        parts = list(parts)
        for k in order:
            parts[k] = lax.ppermute(parts[k], "space", swaps[k])
        return parts

    sent = []
    for chunk in range(CHUNKS):
        info = scalars(grid_at, *project_at)
        sent.append(
            exchange(project_rows(spatial, ordered, project_all, info, chunk * count, count))
        )
    info = scalars(*qkv_at, *out_at)
    gain, bias = as_row(ln_gain), as_row(ln_bias)
    back = [exchange(attend(parts, gain, bias, qkv_all, out_all, info)) for parts in sent]
    result = None
    for chunk in range(CHUNKS):
        result = restore_rows(back[chunk], scalars(grid_at), rows, chunk * count, result)
    return result.reshape(fields.shape)


def solution(mesh):
    in_specs = (
        P("dp", "space", None, None),
        P(),
        P(),
        P(None, "dp"),
        P(),
        P(),
        P(),
        P(None, "dp"),
        P(),
        P(),
        P(None, "dp"),
        P(None, "dp"),
    )
    out_specs = P("dp", "space", None, None)
    return jax.shard_map(local, mesh=mesh, in_specs=in_specs, out_specs=out_specs, check_vma=False)
```

```python
import functools
import math

import jax
import jax.numpy as jnp
from jax import lax
from jax.experimental import pallas as pl
from jax.experimental.pallas import tpu as pltpu
from jax.sharding import PartitionSpec as P

HD = 32
GRID = 8
CHUNKS = 2
ROOT = math.sqrt(2.0 / math.pi)
LIN = 2.0 * ROOT
CUBE = 8.0 * ROOT * 0.044715
F32 = jnp.float32
BF16 = jnp.bfloat16
VMEM_LIMIT = 18 * 1024 * 1024


def half_gelu(half):
    return half + half * jnp.tanh(half * (LIN + CUBE * (half * half)))


def one_hot_order(cols, inverse=False):
    stride = cols // GRID
    row = lax.broadcasted_iota(jnp.int32, (cols, cols), 0)
    col = lax.broadcasted_iota(jnp.int32, (cols, cols), 1)
    if inverse:
        row, col = col, row
    return jnp.where(col == (row % GRID) * stride + row // GRID, 1.0, 0.0).astype(BF16)


def dot(a, b):
    return jnp.dot(a, b, preferred_element_type=F32)


def vmem():
    return pl.BlockSpec(memory_space=pltpu.VMEM)


def smem():
    return pl.BlockSpec(memory_space=pltpu.SMEM)


def params():
    return pltpu.CompilerParams(vmem_limit_bytes=VMEM_LIMIT)


CORE, DP, SPACE, LAST, GROUPS = range(5)


def grid_of(info):
    return info[SPACE] // info[GROUPS]


def cost(flops, moved):
    return pl.CostEstimate(flops=flops, bytes_accessed=moved, transcendentals=flops // 1024)


def share_kernel(info, expand, project, qkv, out, expand_part, project_part, rest_part):
    expand_part[...] = expand[...]
    project_part[...] = project[...]
    width = qkv.shape[1]
    rest_part[:, :width] = qkv[...]
    rest_part[:, width:] = out[...]


def share_weights(info, w_expand, w_project, w_qkv, w_out):
    by_rows = lambda w: pl.BlockSpec((w.shape[0] // 2, w.shape[1]), lambda t, i: (i[CORE], 0))
    by_cols = pl.BlockSpec((w_expand.shape[0], w_expand.shape[1] // 2), lambda t, i: (0, i[CORE]))
    whole = lambda shape: pl.BlockSpec(shape, lambda t, i: (0, 0))
    shapes = [
        (w_expand.shape[0], w_expand.shape[1] // 2),
        (w_project.shape[0] // 2, w_project.shape[1]),
        (w_qkv.shape[0] // 2, w_qkv.shape[1] + w_out.shape[1]),
    ]
    return pl.pallas_call(
        share_kernel,
        grid_spec=pltpu.PrefetchScalarGridSpec(
            num_scalar_prefetch=1,
            grid=(1,),
            in_specs=[by_cols, by_rows(w_project), by_rows(w_qkv), by_rows(w_out)],
            out_specs=[whole(shape) for shape in shapes],
        ),
        out_shape=[jax.ShapeDtypeStruct(shape, BF16) for shape in shapes],
        compiler_params=params(),
        name="share_weights",
    )(info, w_expand, w_project, w_qkv, w_out)


def order_kernel(image, above, below, scale, shift, ordered, normed):
    rows, cols, _ = image.shape
    pick = one_hot_order(cols)
    for row in range(rows + 2):
        if row == 0:
            placed = dot(pick, above[0])
        elif row == rows + 1:
            placed = dot(pick, below[0])
        else:
            placed = dot(pick, image[row - 1])
            ordered[row - 1] = placed.astype(BF16)
        normed[row * cols : (row + 1) * cols, :] = (
            placed * (0.5 * scale[...]) + 0.5 * shift[...]
        ).astype(BF16)


def expand_kernel(first, info, *refs):
    refs = list(refs)
    take = lambda n: [refs.pop(0) for _ in range(n)]
    if first:
        sources = take(5)
    else:
        (normed,) = take(1)
    weight, bias, taps, tap_bias = take(4)
    if first:
        out, ordered, normed = take(3)
    else:
        _, out = take(2)
    raw, wide = refs
    cols = wide.shape[1] - 2 * GRID
    rows = wide.shape[0] - 2
    width = bias.shape[-1]

    if first:

        @pl.when(pl.program_id(0) == 0)
        def _():
            order_kernel(*sources, ordered, normed)

    half_bias = 0.5 * bias[...]
    half_taps = 0.5 * taps[...]
    half_tap_bias = 0.5 * tap_bias[...]
    lane = lax.broadcasted_iota(jnp.int32, (GRID, width), 0)
    batch = (rows + 2) // 2 * cols
    for start in range(0, (rows + 2) * cols, batch):
        raw[start : start + batch, :] = dot(normed[start : start + batch, :], weight[...])
    for row in range(rows + 2):
        value = half_gelu(raw[row * cols : (row + 1) * cols, :] + half_bias)
        if row == 0:
            value = value * jnp.where(info[SPACE] > 0, 1.0, 0.0)
        elif row == rows + 1:
            value = value * jnp.where(info[SPACE] < info[LAST], 1.0, 0.0)
        wide[row, GRID : GRID + cols, :] = value
        head = value[:GRID]
        tail = value[cols - GRID :]
        wide[row, :GRID, :] = jnp.where(lane == 0, 0.0, pltpu.roll(tail, 1, 0))
        wide[row, GRID + cols :, :] = jnp.where(
            lane == GRID - 1, 0.0, pltpu.roll(head, GRID - 1, 0)
        )
        if row >= 2:
            total = half_tap_bias
            for row_off in range(3):
                for col_off in range(3):
                    total = (
                        total
                        + wide[row - 2 + row_off, GRID * col_off : GRID * col_off + cols, :]
                        * half_taps[row_off, col_off][None]
                    )
            out[(row - 2) * cols : (row - 1) * cols, :] = half_gelu(total).astype(BF16)


def expand_some(info, sources, weight, bias, taps, tap_bias, tile_of, spatial):
    first = spatial is None
    chans, here = weight.shape
    inner = bias.shape[-1]
    width = min(256, here)
    if first:
        rows, cols, _ = sources[0].shape
    else:
        rows, cols = spatial[1:]
    whole = lambda shape: pl.BlockSpec(shape, lambda t, info: (0,) * len(shape))
    in_specs = [whole(s.shape) for s in sources]
    in_specs += [
        pl.BlockSpec((chans, width), lambda t, info: (0, t)),
        pl.BlockSpec((1, width), lambda t, info: (0, tile_of(info, t))),
        pl.BlockSpec((3, 3, width), lambda t, info: (0, 0, tile_of(info, t))),
        pl.BlockSpec((1, width), lambda t, info: (0, tile_of(info, t))),
    ]
    operands = [info, *sources, weight, bias, taps, tap_bias]
    out_specs = [pl.BlockSpec((rows * cols, width), lambda t, info: (0, tile_of(info, t)))]
    out_shape = [jax.ShapeDtypeStruct((rows * cols, inner), BF16)]
    aliases = {}
    if first:
        shapes = [(rows, cols, chans), ((rows + 2) * cols, chans)]
        out_specs += [whole(shape) for shape in shapes]
        out_shape += [jax.ShapeDtypeStruct(shape, BF16) for shape in shapes]
    else:
        in_specs.append(pl.BlockSpec(memory_space=pl.ANY))
        aliases = {len(operands): 0}
        operands.append(spatial[0])
    return pl.pallas_call(
        functools.partial(expand_kernel, first),
        grid_spec=pltpu.PrefetchScalarGridSpec(
            num_scalar_prefetch=1,
            grid=(here // width,),
            in_specs=in_specs,
            out_specs=out_specs,
            scratch_shapes=[
                pltpu.VMEM(((rows + 2) * cols, width), F32),
                pltpu.VMEM((rows + 2, cols + 2 * GRID, width), F32),
            ],
        ),
        out_shape=out_shape,
        input_output_aliases=aliases,
        compiler_params=params(),
        cost_estimate=cost(2 * rows * cols * chans * here, 1 << 22),
        name="expand_conv",
    )(*operands)


def pieced_dot(lhs, pieces, info, put):
    own = pieces[0]
    width = own.shape[1]
    if len(pieces) == 1:
        put(0, width, dot(lhs[...], own[...]))
        return
    mine = info[DP]
    put(pl.multiple_of(mine * width, width), width, dot(lhs[...], own[...]))
    total = None
    for n, piece in enumerate(pieces[1:]):
        depth = piece.shape[0]
        at = info[CORE] if n == 0 else 1 - info[CORE]
        span = pl.ds(pl.multiple_of(at * depth, depth), depth)
        part = dot(lhs[:, span], piece[...])
        total = part if total is None else total + part
    put(pl.multiple_of((1 - mine) * width, width), width, total)


def project_kernel(pieces, info, spatial, ordered, *refs):
    weights = refs[:pieces]
    outs = refs[pieces : pieces + GRID]
    (conv,) = refs[pieces + GRID :]
    count, cols, chans = ordered.shape
    size = outs[0].shape[1]

    def put(start, width, product):
        span = pl.ds(start, width)
        for row in range(count):
            at = slice(row * cols, (row + 1) * cols)
            conv[at, span] = (ordered[row, :, span].astype(F32) + product[at]).astype(BF16)

    pieced_dot(spatial, weights, info, put)
    mine = grid_of(info)
    for k in range(GRID):
        start = pl.multiple_of((mine ^ k) * size, size)
        for row in range(count):
            outs[k][row] = conv[pl.ds(row * cols + start, size), :]


def project_rows(info, spatial, ordered, weights, chunk, count):
    rows, cols, chans = ordered.shape
    inner = spatial.shape[1]
    size = cols // GRID
    out = jax.ShapeDtypeStruct((count, size, chans), BF16)
    whole = lambda shape: pl.BlockSpec(shape, lambda t, info: (0,) * len(shape))
    return pl.pallas_call(
        functools.partial(project_kernel, len(weights)),
        grid_spec=pltpu.PrefetchScalarGridSpec(
            num_scalar_prefetch=1,
            grid=(1,),
            in_specs=[
                pl.BlockSpec((count * cols, inner), lambda t, info: (chunk, 0)),
                pl.BlockSpec((count, cols, chans), lambda t, info: (chunk, 0, 0)),
            ]
            + [whole(w.shape) for w in weights],
            out_specs=[whole(out.shape)] * GRID,
            scratch_shapes=[pltpu.VMEM((count * cols, chans), BF16)],
        ),
        out_shape=[out] * GRID,
        compiler_params=params(),
        cost_estimate=cost(2 * count * cols * inner * chans, 1 << 22),
        name="project_rows",
    )(info, spatial, ordered, *weights)


def attend_kernel(pieces, info, gain, bias, *refs):
    refs = list(refs)
    take = lambda n: [refs.pop(0) for _ in range(n)]
    qkv_pieces, out_pieces, rest = take(1), take(1), take(pieces - 1)
    split = qkv_pieces[0].shape[1]
    for both in rest:
        qkv_pieces.append(both.at[:, :split])
        out_pieces.append(both.at[:, split:])
    tokens, outs = take(GRID), take(GRID)
    lned, triple, mixed, resid = refs
    count, size, chans = tokens[0].shape
    wins = size // GRID
    length = GRID * GRID
    group = min(256, chans)
    heads = group // HD
    keys = heads * length

    for a in range(count):
        rows = [tokens[k][a].astype(F32) for k in range(GRID)]
        for w in range(wins):
            x = jnp.concatenate([r[w * GRID : (w + 1) * GRID] for r in rows], axis=0)
            start = (a * wins + w) * length
            resid[start : start + length, :] = x
            center = jnp.mean(x, axis=-1, keepdims=True)
            off = x - center
            spread = jnp.mean(off * off, axis=-1, keepdims=True)
            lned[start : start + length, :] = (
                off * lax.rsqrt(spread + 1e-05) * gain[...] + bias[...]
            ).astype(BF16)

    def put_triple(start, width, product):
        triple[:, pl.ds(start, width)] = product.astype(BF16)

    pieced_dot(lned, qkv_pieces, info, put_triple)

    def same(shape, row_block, col_block):
        row = lax.broadcasted_iota(jnp.int32, shape, 0) // row_block
        col = lax.broadcasted_iota(jnp.int32, shape, 1) // col_block
        return jnp.where(row == col, 1.0, 0.0).astype(BF16)

    spread_mask = same((keys, group), length, HD)
    sum_mask = same((256, 256), length, length)
    factor = math.log2(math.e) / math.sqrt(HD)
    for win in range(count * wins):
        at = slice(win * length, (win + 1) * length)
        for g in range(chans // group):
            cols = slice(g * group, (g + 1) * group)
            query = triple[at, cols]
            key = triple[at, chans + g * group : chans + (g + 1) * group]
            value = triple[at, 2 * chans + g * group : 2 * chans + (g + 1) * group]
            key_wide = jnp.concatenate([key] * heads, axis=0) * spread_mask
            value_wide = jnp.concatenate([value] * heads, axis=0) * spread_mask
            scores = lax.dot_general(
                query, key_wide, (((1,), (1,)), ((), ())), preferred_element_type=F32
            )
            exponent = jnp.minimum(jnp.exp2(scores * factor), 3.3895e38)
            rounded = exponent.astype(BF16)
            sums = jnp.concatenate(
                [dot(rounded[:, n : n + 256], sum_mask) for n in range(0, keys, 256)], axis=1
            )
            soft = (exponent / sums).astype(BF16)
            mixed[at, cols] = dot(soft, value_wide).astype(BF16)

    def put_out(start, width, product):
        span = pl.ds(start, width)
        resid[:, span] = resid[:, span] + product

    pieced_dot(mixed, out_pieces, info, put_out)
    for a in range(count):
        for k in range(GRID):
            parts = []
            for w in range(wins):
                start = (a * wins + w) * length + k * GRID
                parts.append(resid[start : start + GRID, :])
            outs[k][a] = jnp.concatenate(parts, axis=0).astype(BF16)


def attend(info, tokens, gain, bias, w_qkv, w_out, rest):
    count, size, chans = tokens[0].shape
    total = count * size * GRID
    out = jax.ShapeDtypeStruct(tokens[0].shape, BF16)
    return pl.pallas_call(
        functools.partial(attend_kernel, 1 + len(rest)),
        out_shape=[out] * GRID,
        in_specs=[smem()] + [vmem()] * (4 + len(rest) + GRID),
        out_specs=[vmem()] * GRID,
        scratch_shapes=[
            pltpu.VMEM((total, chans), BF16),
            pltpu.VMEM((total, 3 * chans), BF16),
            pltpu.VMEM((total, chans), BF16),
            pltpu.VMEM((total, chans), F32),
        ],
        compiler_params=params(),
        cost_estimate=cost(16 * total * chans * chans, 1 << 22),
        name="attend",
    )(info, gain, bias, w_qkv, w_out, *rest, *tokens)


def restore_kernel(info, *refs):
    parts = refs[:GRID]
    out, buf = refs[-2:]
    count, cols, _ = out.shape
    size = parts[0].shape[1]
    back = one_hot_order(cols, inverse=True)
    mine = grid_of(info)
    for row in range(count):
        for k in range(GRID):
            at = pl.ds(row * cols + pl.multiple_of((mine ^ k) * size, size), size)
            buf[at, :] = parts[k][row]
        out[row] = dot(back, buf[row * cols : (row + 1) * cols, :]).astype(BF16)


def restore_rows(info, parts, rows, chunk, out):
    count, size, chans = parts[0].shape
    cols = size * GRID
    in_specs = [pl.BlockSpec((count, size, chans), lambda t, info: (0, 0, 0))] * GRID
    operands = [info, *parts]
    aliases = {}
    if out is not None:
        in_specs.append(pl.BlockSpec(memory_space=pl.ANY))
        aliases = {len(operands): 0}
        operands.append(out)
    return pl.pallas_call(
        restore_kernel,
        grid_spec=pltpu.PrefetchScalarGridSpec(
            num_scalar_prefetch=1,
            grid=(1,),
            in_specs=in_specs,
            out_specs=pl.BlockSpec((count, cols, chans), lambda t, info: (chunk, 0, 0)),
            scratch_shapes=[pltpu.VMEM((count * cols, chans), BF16)],
        ),
        out_shape=jax.ShapeDtypeStruct((rows, cols, chans), BF16),
        input_output_aliases=aliases,
        compiler_params=params(),
        cost_estimate=cost(2 * count * cols * cols * chans, 1 << 21),
        name="restore_rows",
    )(*operands)


def after(value, *others):
    return lax.optimization_barrier((value, *others))[0]


def local(
    fields,
    bn_scale,
    bn_shift,
    w_expand,
    expand_bias,
    dw_kernel,
    dw_bias,
    w_project,
    ln_gain,
    ln_bias,
    w_qkv,
    w_out,
):
    _, rows, cols, chans = fields.shape
    dp, space = lax.axis_size("dp"), lax.axis_size("space")
    dp_at, space_at = lax.axis_index("dp"), lax.axis_index("space")
    groups = space // GRID
    pairs = dp == 2 and space % 2 == 0
    info = jnp.stack(
        [
            jnp.asarray(v, jnp.int32)
            for v in (space_at % 2, dp_at, space_at, space - 1, groups)
        ]
    )
    as_row = lambda v: v.reshape(1, -1)
    image = fields.reshape(rows, cols, chans)
    small = (as_row(expand_bias), dw_kernel, as_row(dw_bias))
    gain, bias = as_row(ln_gain), as_row(ln_bias)

    over_dp = lambda w: lax.ppermute(w, "dp", [(0, 1), (1, 0)])
    over_core = lambda w: lax.ppermute(w, "space", [(i, i ^ 1) for i in range(space)])
    if pairs:
        mine = share_weights(info, w_expand, w_project, w_qkv, w_out)
        expand_got = over_dp(mine[0])
    above = lax.ppermute(image[rows - 1 :], "space", [(i, i + 1) for i in range(space - 1)])
    below = lax.ppermute(image[:1], "space", [(i + 1, i) for i in range(space - 1)])
    sources = (image, above, below, as_row(bn_scale), as_row(bn_shift))
    if pairs:
        project_got = over_dp(mine[1])
        rest_got = over_dp(mine[2])
        tiles = max(1, w_expand.shape[1] // 256)
        spatial, ordered, normed = expand_some(
            info, sources, w_expand, *small, lambda i, t: i[DP] * tiles + t, None
        )
        half = tiles // 2
        expand_got = after(expand_got, spatial)
        expand_other = over_core(expand_got)
        (spatial,) = expand_some(
            info,
            (normed,),
            expand_got,
            *small,
            lambda i, t: (1 - i[DP]) * tiles + i[CORE] * half + t,
            (spatial, rows, cols),
        )
        (spatial,) = expand_some(
            info,
            (normed,),
            expand_other,
            *small,
            lambda i, t: (1 - i[DP]) * tiles + (1 - i[CORE]) * half + t,
            (spatial, rows, cols),
        )
        project_got = after(project_got, expand_other)
        project_all = [w_project, project_got, over_core(project_got)]
    else:
        gathered = lambda w: lax.all_gather(w, "dp", axis=1, tiled=True)
        spatial, ordered, normed = expand_some(
            info, sources, gathered(w_expand), *small, lambda i, t: t, None
        )
        project_all = [gathered(w_project)]
        w_qkv, w_out, rest = gathered(w_qkv), gathered(w_out), []

    count = rows // CHUNKS
    swaps = [
        [(s, (((s // groups) ^ k) * groups) + s % groups) for s in range(space)]
        for k in range(GRID)
    ]
    order = (4, 6, 5, 7, 2, 3, 1)

    def exchange(parts):
        parts = list(parts)
        for k in order:
            parts[k] = lax.ppermute(parts[k], "space", swaps[k])
        return parts

    sent = []
    for chunk in range(CHUNKS):
        sent.append(
            exchange(project_rows(info, spatial, ordered, project_all, chunk, count))
        )
    if pairs:
        rest_got = after(rest_got, spatial)
        rest = [rest_got, over_core(rest_got)]
    back = [exchange(attend(info, parts, gain, bias, w_qkv, w_out, rest)) for parts in sent]
    result = None
    for chunk in range(CHUNKS):
        result = restore_rows(info, back[chunk], rows, chunk, result)
    return result.reshape(fields.shape)


def solution(mesh):
    in_specs = (
        P("dp", "space", None, None),
        P(),
        P(),
        P(None, "dp"),
        P(),
        P(),
        P(),
        P(None, "dp"),
        P(),
        P(),
        P(None, "dp"),
        P(None, "dp"),
    )
    out_specs = P("dp", "space", None, None)
    return jax.shard_map(local, mesh=mesh, in_specs=in_specs, out_specs=out_specs, check_vma=False)
```

```python
import functools
import math

import jax
import jax.numpy as jnp
from jax import lax
from jax.experimental import pallas as pl
from jax.experimental.pallas import tpu as pltpu
from jax.sharding import PartitionSpec as P

HD = 32
GRID = 8
CHUNKS = 1
SPLIT = (True,)
ORDER = (4, 6, 5, 7, 2, 3, 1)
ROOT = math.sqrt(2.0 / math.pi)
LIN = 2.0 * ROOT
CUBE = 8.0 * ROOT * 0.044715
F32 = jnp.float32
BF16 = jnp.bfloat16
VMEM_LIMIT = 18 * 1024 * 1024


def half_gelu(half):
    return half + half * jnp.tanh(half * (LIN + CUBE * (half * half)))


def one_hot_order(cols, inverse=False):
    stride = cols // GRID
    row = lax.broadcasted_iota(jnp.int32, (cols, cols), 0)
    col = lax.broadcasted_iota(jnp.int32, (cols, cols), 1)
    if inverse:
        row, col = col, row
    return jnp.where(col == (row % GRID) * stride + row // GRID, 1.0, 0.0).astype(BF16)


def dot(a, b):
    return jnp.dot(a, b, preferred_element_type=F32)


def vmem():
    return pl.BlockSpec(memory_space=pltpu.VMEM)


def smem():
    return pl.BlockSpec(memory_space=pltpu.SMEM)


def hbm():
    return pl.BlockSpec(memory_space=pltpu.HBM)


def in_hbm(array):
    return pltpu.with_memory_space_constraint(array, pltpu.HBM)


def any_space():
    return pl.BlockSpec(memory_space=pl.ANY)


def params():
    return pltpu.CompilerParams(vmem_limit_bytes=VMEM_LIMIT)


CORE, DP, SPACE, LAST, GROUPS = range(5)


def grid_of(info):
    return info[SPACE] // info[GROUPS]


def cost():
    return pl.CostEstimate(flops=1, bytes_accessed=1, transcendentals=1)


def copy_all(pairs, sems):
    copies = [pltpu.make_async_copy(src, dst, sems.at[n]) for n, (src, dst) in enumerate(pairs)]
    for copy in copies:
        copy.start()
    return copies


def edges_kernel(image, top, bottom, sems):
    rows = image.shape[0]
    for copy in copy_all([(image.at[rows - 1 : rows], bottom), (image.at[0:1], top)], sems):
        copy.wait()


def edge_rows(image):
    edge = jax.ShapeDtypeStruct((1,) + image.shape[1:], BF16)
    return pl.pallas_call(
        edges_kernel,
        in_specs=[hbm()],
        out_specs=[any_space()] * 2,
        out_shape=[edge, edge],
        scratch_shapes=[pltpu.SemaphoreType.DMA((2,))],
        compiler_params=params(),
        name="edge_rows",
    )(in_hbm(image))


def shares_kernel(info, expand, project, expand_part, project_part, sems):
    def span(part, axis):
        size = part.shape[axis]
        return pl.ds(pl.multiple_of(info[CORE] * size, size), size)

    moves = [
        (expand.at[:, span(expand_part, 1)], expand_part),
        (project.at[span(project_part, 0)], project_part),
    ]
    for copy in copy_all(moves, sems):
        copy.wait()


def share_weights(info, w_expand, w_project):
    shapes = [
        (w_expand.shape[0], w_expand.shape[1] // 2),
        (w_project.shape[0] // 2, w_project.shape[1]),
    ]
    return pl.pallas_call(
        shares_kernel,
        in_specs=[smem(), hbm(), hbm()],
        out_specs=[vmem()] * 2,
        out_shape=[jax.ShapeDtypeStruct(shape, BF16) for shape in shapes],
        scratch_shapes=[pltpu.SemaphoreType.DMA((2,))],
        compiler_params=params(),
        name="share_weights",
    )(info, *map(in_hbm, (w_expand, w_project)))


def order_kernel(image, above, below, scale, shift, ordered, normed):
    rows, cols, _ = image.shape
    pick = one_hot_order(cols)
    for row in range(rows + 2):
        if row == 0:
            placed = dot(pick, above[0])
        elif row == rows + 1:
            placed = dot(pick, below[0])
        else:
            placed = dot(pick, image[row - 1])
            ordered[row - 1] = placed.astype(BF16)
        normed[row] = (
            placed * (0.5 * scale[...]) + 0.5 * shift[...]
        ).astype(BF16)


def expand_kernel(first, tile_of, info, *refs):
    refs = list(refs)
    take = lambda n: [refs.pop(0) for _ in range(n)]
    step = pl.program_id(0)
    if first:
        image, above, below, scale, shift, weight, bias, taps, tap_bias = take(9)
        out, ordered, normed = take(3)
        raw, wide, sems, *held = refs
        moved = [(image, held[0])]
        moved += list(zip((scale, shift, weight, bias, taps, tap_bias), held[1:]))
        image, scale, shift, weight, bias, taps, tap_bias = held

        @pl.when(step == 0)
        def _():
            copies = copy_all(moved, sems)
            for copy in copies:
                copy.wait()
            order_kernel(image, above, below, scale, shift, ordered, normed)

    else:
        normed, weight, bias, taps, tap_bias, out, raw, wide = refs
    width = raw.shape[1]
    cols = wide.shape[1] - 2 * GRID
    rows = wide.shape[0] - 2
    if first:
        here = pl.ds(pl.multiple_of(step * width, width), width)
        tile = pl.ds(pl.multiple_of(tile_of(info, step) * width, width), width)
    else:
        here = tile = slice(None)
    weight = weight[:, here]
    half_bias = 0.5 * bias[:, tile]
    half_taps = 0.5 * taps[:, :, tile]
    half_tap_bias = 0.5 * tap_bias[:, tile]
    lane = lax.broadcasted_iota(jnp.int32, (GRID, width), 0)
    batch = (rows + 2) // 2
    for row in range(0, rows + 2, batch):
        tokens = normed[row : row + batch].reshape(batch * cols, -1)
        raw[row * cols : (row + batch) * cols, :] = dot(tokens, weight)
    for row in range(rows + 2):
        value = half_gelu(raw[row * cols : (row + 1) * cols, :] + half_bias)
        if row == 0:
            value = value * jnp.where(info[SPACE] > 0, 1.0, 0.0)
        elif row == rows + 1:
            value = value * jnp.where(info[SPACE] < info[LAST], 1.0, 0.0)
        wide[row, GRID : GRID + cols, :] = value
        head = value[:GRID]
        tail = value[cols - GRID :]
        wide[row, :GRID, :] = jnp.where(lane == 0, 0.0, pltpu.roll(tail, 1, 0))
        wide[row, GRID + cols :, :] = jnp.where(
            lane == GRID - 1, 0.0, pltpu.roll(head, GRID - 1, 0)
        )
        if row >= 2:
            total = half_tap_bias
            for row_off in range(3):
                for col_off in range(3):
                    total = (
                        total
                        + wide[row - 2 + row_off, GRID * col_off : GRID * col_off + cols, :]
                        * half_taps[row_off, col_off][None]
                    )
            out[(row - 2) * cols : (row - 1) * cols, :] = half_gelu(total).astype(BF16)


def expand_some(info, sources, weight, bias, taps, tap_bias, tile_of, first):
    chans, here = weight.shape
    width = min(256, here)
    if first:
        rows, cols, _ = sources[0].shape
    else:
        rows, cols = sources[0].shape[0] - 2, sources[0].shape[1]
    whole = lambda shape: pl.BlockSpec(shape, lambda t, info: (0,) * len(shape))
    held = []
    if first:
        in_specs = [hbm(), whole(sources[1].shape), whole(sources[2].shape)] + [hbm()] * 6
        fetched = [sources[0], *sources[3:], weight, bias, taps, tap_bias]
        held = [pltpu.SemaphoreType.DMA((len(fetched),))]
        held += [pltpu.VMEM(f.shape, f.dtype) for f in fetched]
    else:
        in_specs = [whole(s.shape) for s in sources]
        in_specs += [
            pl.BlockSpec((chans, width), lambda t, info: (0, t)),
            pl.BlockSpec((1, width), lambda t, info: (0, tile_of(info, t))),
            pl.BlockSpec((3, 3, width), lambda t, info: (0, 0, tile_of(info, t))),
            pl.BlockSpec((1, width), lambda t, info: (0, tile_of(info, t))),
        ]
    operands = [info, *sources, weight, bias, taps, tap_bias]
    if first:
        operands = [o if n in (0, 2, 3) else in_hbm(o) for n, o in enumerate(operands)]
    out_specs = [pl.BlockSpec((rows * cols, width), lambda t, info: (0, t))]
    out_shape = [jax.ShapeDtypeStruct((rows * cols, here), BF16)]
    if first:
        shapes = [(rows, cols, chans), (rows + 2, cols, chans)]
        out_specs += [whole(shape) for shape in shapes]
        out_shape += [jax.ShapeDtypeStruct(shape, BF16) for shape in shapes]
    return pl.pallas_call(
        functools.partial(expand_kernel, first, tile_of),
        grid_spec=pltpu.PrefetchScalarGridSpec(
            num_scalar_prefetch=1,
            grid=(here // width,),
            in_specs=in_specs,
            out_specs=out_specs,
            scratch_shapes=[
                pltpu.VMEM(((rows + 2) * cols, width), F32),
                pltpu.VMEM((rows + 2, cols + 2 * GRID, width), F32),
                *held,
            ],
        ),
        out_shape=out_shape,
        compiler_params=params(),
        cost_estimate=cost(),
        name="expand_conv",
    )(*operands)


def pieced_dot(lhs, pieces, info, put):
    width = pieces[0].shape[1]
    for n, piece in enumerate(pieces):
        if len(pieces) == 1:
            start = 0
        else:
            start = pl.multiple_of((1 - info[DP] if n else info[DP]) * width, width)
        put(start, width, dot(lhs[...], piece[...]))


def project_kernel(pieces, split, info, ordered, *refs):
    refs = list(refs)
    take = lambda n: [refs.pop(0) for _ in range(n)]
    spatial, weights, outs, (conv, other) = take(pieces), take(pieces), take(GRID if split else 1), refs
    count, cols, chans = ordered.shape
    size = cols // GRID
    own = weights[0]
    width = own.shape[1]

    def put(start, product):
        span = pl.ds(start, width)
        for row in range(count):
            at = slice(row * cols, (row + 1) * cols)
            conv[at, span] = (ordered[row, :, span].astype(F32) + product[at]).astype(BF16)

    if pieces == 1:
        put(0, dot(spatial[0][...], own[...]))
    else:
        mine, core = info[DP], info[CORE]
        half = own.shape[0] // 2
        for n, at in ((1, core), (2, 1 - core)):
            other[pl.ds(pl.multiple_of(at * half, half), half), :] = weights[n][...]
        part = half // 2
        starts = (
            (mine * half, half),
            ((1 - mine) * half + core * part, part),
            ((1 - mine) * half + (1 - core) * part, part),
        )
        for weight, column in ((own, mine), (other, 1 - mine)):
            total = None
            for lhs, (start, depth) in zip(spatial, starts):
                rows = pl.ds(pl.multiple_of(start, part), depth)
                product = dot(lhs[...], weight[rows, :])
                total = product if total is None else total + product
            put(pl.multiple_of(column * width, width), total)

    for k in range(GRID):
        place = (grid_of(info) ^ k) if split else k
        for row in range(count):
            start = row * cols + pl.multiple_of(place * size, size)
            block_of(outs, k)[row] = conv[pl.ds(start, size), :]


def block_of(parts, k):
    return parts[k] if len(parts) > 1 else parts[0].at[k]


def project_rows(info, spatial, ordered, weights, chunk, count, split):
    rows, cols, chans = ordered.shape
    size = cols // GRID
    block = (count, size, chans)
    outs = [block] * GRID if split else [(GRID,) + block]
    whole = lambda shape: pl.BlockSpec(shape, lambda t, info: (0,) * len(shape))
    return pl.pallas_call(
        functools.partial(project_kernel, len(weights), split),
        grid_spec=pltpu.PrefetchScalarGridSpec(
            num_scalar_prefetch=1,
            grid=(1,),
            in_specs=[pl.BlockSpec((count, cols, chans), lambda t, info: (chunk, 0, 0))]
            + [pl.BlockSpec((count * cols, s.shape[1]), lambda t, info: (chunk, 0)) for s in spatial]
            + [whole(w.shape) for w in weights],
            out_specs=[whole(out) for out in outs],
            scratch_shapes=[pltpu.VMEM((count * cols, chans), BF16), pltpu.VMEM(weights[0].shape, BF16)],
        ),
        out_shape=[jax.ShapeDtypeStruct(out, BF16) for out in outs],
        compiler_params=params(),
        cost_estimate=cost(),
        name="project_rows",
    )(info, ordered, *spatial, *weights)


def attend_kernel(pieces, blocks, info, gain, bias, *refs):
    refs = list(refs)
    take = lambda n: [refs.pop(0) for _ in range(n)]
    qkv_pieces, out_pieces = take(pieces), take(pieces)
    tokens, outs = take(blocks), take(blocks)
    lned, triple, mixed, resid = refs
    count, size, chans = tokens[0].shape[-3:]
    wins = size // GRID
    length = GRID * GRID
    group = min(256, chans)
    heads = group // HD
    keys = heads * length

    for a in range(count):
        rows = [block_of(tokens, k)[a].astype(F32) for k in range(GRID)]
        for w in range(wins):
            x = jnp.concatenate([r[w * GRID : (w + 1) * GRID] for r in rows], axis=0)
            start = (a * wins + w) * length
            resid[start : start + length, :] = x
            center = jnp.mean(x, axis=-1, keepdims=True)
            off = x - center
            spread = jnp.mean(off * off, axis=-1, keepdims=True)
            lned[start : start + length, :] = (
                off * lax.rsqrt(spread + 1e-05) * gain[...] + bias[...]
            ).astype(BF16)

    def put_triple(start, width, product):
        triple[:, pl.ds(start, width)] = product.astype(BF16)

    pieced_dot(lned, qkv_pieces, info, put_triple)

    def same(shape, row_block, col_block):
        row = lax.broadcasted_iota(jnp.int32, shape, 0) // row_block
        col = lax.broadcasted_iota(jnp.int32, shape, 1) // col_block
        return jnp.where(row == col, 1.0, 0.0).astype(BF16)

    spread_mask = same((keys, group), length, HD)
    sum_mask = same((256, 256), length, length)
    factor = math.log2(math.e) / math.sqrt(HD)
    for win in range(count * wins):
        at = slice(win * length, (win + 1) * length)
        for g in range(chans // group):
            cols = slice(g * group, (g + 1) * group)
            query = triple[at, cols]
            key = triple[at, chans + g * group : chans + (g + 1) * group]
            value = triple[at, 2 * chans + g * group : 2 * chans + (g + 1) * group]
            key_wide = jnp.concatenate([key] * heads, axis=0) * spread_mask
            value_wide = jnp.concatenate([value] * heads, axis=0) * spread_mask
            scores = lax.dot_general(
                query, key_wide, (((1,), (1,)), ((), ())), preferred_element_type=F32
            )
            exponent = jnp.minimum(jnp.exp2(scores * factor), 3.3895e38)
            rounded = exponent.astype(BF16)
            sums = jnp.concatenate(
                [dot(rounded[:, n : n + 256], sum_mask) for n in range(0, keys, 256)], axis=1
            )
            soft = (exponent / sums).astype(BF16)
            mixed[at, cols] = dot(soft, value_wide).astype(BF16)

    def put_out(start, width, product):
        span = pl.ds(start, width)
        resid[:, span] = resid[:, span] + product

    pieced_dot(mixed, out_pieces, info, put_out)
    for a in range(count):
        for k in range(GRID):
            parts = []
            for w in range(wins):
                start = (a * wins + w) * length + k * GRID
                parts.append(resid[start : start + GRID, :])
            block_of(outs, k)[a] = jnp.concatenate(parts, axis=0).astype(BF16)


def attend(info, tokens, gain, bias, w_qkv, w_out):
    count, size, chans = tokens[0].shape[-3:]
    total = count * size * GRID
    return pl.pallas_call(
        functools.partial(attend_kernel, len(w_qkv), len(tokens)),
        out_shape=[jax.ShapeDtypeStruct(t.shape, BF16) for t in tokens],
        in_specs=[smem()] + [vmem()] * (2 + 2 * len(w_qkv) + len(tokens)),
        out_specs=[vmem()] * len(tokens),
        scratch_shapes=[
            pltpu.VMEM((total, chans), BF16),
            pltpu.VMEM((total, 3 * chans), BF16),
            pltpu.VMEM((total, chans), BF16),
            pltpu.VMEM((total, chans), F32),
        ],
        compiler_params=params(),
        cost_estimate=cost(),
        name="attend",
    )(info, gain, bias, *w_qkv, *w_out, *tokens)


def restore_kernel(blocks, info, *refs):
    parts = refs[:blocks]
    out, buf = refs[-2:]
    count, cols, chans = out.shape
    size = cols // GRID
    back = one_hot_order(cols, inverse=True)
    for row in range(count):
        if blocks == 1:
            tokens = parts[0][:, row].reshape(cols, chans)
        else:
            for k in range(GRID):
                place = pl.multiple_of((grid_of(info) ^ k) * size, size)
                buf[pl.ds(row * cols + place, size), :] = parts[k][row]
            tokens = buf[row * cols : (row + 1) * cols, :]
        out[row] = dot(back, tokens).astype(BF16)


def restore_rows(info, parts, rows, chunk, out):
    count, size, chans = parts[0].shape[-3:]
    cols = size * GRID
    in_specs = [pl.BlockSpec(p.shape, lambda t, i, n=p.ndim: (0,) * n) for p in parts]
    operands = [info, *parts]
    aliases = {}
    if out is not None:
        in_specs.append(pl.BlockSpec(memory_space=pl.ANY))
        aliases = {len(operands): 0}
        operands.append(out)
    return pl.pallas_call(
        functools.partial(restore_kernel, len(parts)),
        grid_spec=pltpu.PrefetchScalarGridSpec(
            num_scalar_prefetch=1,
            grid=(1,),
            in_specs=in_specs,
            out_specs=pl.BlockSpec((count, cols, chans), lambda t, info: (chunk, 0, 0)),
            scratch_shapes=[pltpu.VMEM((count * cols, chans), BF16)],
        ),
        out_shape=jax.ShapeDtypeStruct((rows, cols, chans), BF16),
        input_output_aliases=aliases,
        compiler_params=params(),
        cost_estimate=cost(),
        name="restore_rows",
    )(*operands)


def after(value, *others):
    return lax.optimization_barrier((value, *others))[0]


def local(
    fields,
    bn_scale,
    bn_shift,
    w_expand,
    expand_bias,
    dw_kernel,
    dw_bias,
    w_project,
    ln_gain,
    ln_bias,
    w_qkv,
    w_out,
):
    _, rows, cols, chans = fields.shape
    dp, space = lax.axis_size("dp"), lax.axis_size("space")
    dp_at, space_at = lax.axis_index("dp"), lax.axis_index("space")
    groups = space // GRID
    pairs = dp == 2 and space % 2 == 0
    info = jnp.stack(
        [
            jnp.asarray(v, jnp.int32)
            for v in (space_at % 2, dp_at, space_at, space - 1, groups)
        ]
    )
    as_row = lambda v: v.reshape(1, -1)
    image = fields.reshape(rows, cols, chans)
    small = (as_row(expand_bias), dw_kernel, as_row(dw_bias))
    gain, bias = as_row(ln_gain), as_row(ln_bias)

    over_dp = lambda w: lax.ppermute(w, "dp", [(0, 1), (1, 0)])
    over_core = lambda w: lax.ppermute(w, "space", [(i, i ^ 1) for i in range(space)])
    top, bottom = edge_rows(image)
    above = lax.ppermute(bottom, "space", [(i, i + 1) for i in range(space - 1)])
    below = lax.ppermute(top, "space", [(i + 1, i) for i in range(space - 1)])
    if pairs:
        mine = share_weights(after(info, top), w_expand, w_project)
        expand_got, project_got = map(over_dp, mine)
        above = after(above, *mine)
    sources = (image, above, below, as_row(bn_scale), as_row(bn_shift))
    if pairs:
        tiles = max(1, w_expand.shape[1] // 256)
        half = tiles // 2
        own_place = lambda i, t: i[DP] * tiles + t
        got_place = lambda i, t: (1 - i[DP]) * tiles + i[CORE] * half + t
        other_place = lambda i, t: (1 - i[DP]) * tiles + (1 - i[CORE]) * half + t
        own, ordered, normed = expand_some(info, sources, w_expand, *small, own_place, True)
        expand_got = after(expand_got, own)
        expand_other = over_core(expand_got)
        (got,) = expand_some(info, (normed,), expand_got, *small, got_place, False)
        expand_other, normed = lax.optimization_barrier((expand_other, normed, got))[:2]
        (other,) = expand_some(info, (normed,), expand_other, *small, other_place, False)
        spatial = [own, got, other]
        project_got = after(project_got, own)
        project_all = [w_project, project_got, over_core(project_got)]
    else:
        gathered = lambda w: lax.all_gather(w, "dp", axis=1, tiled=True)
        spatial, ordered, _ = expand_some(
            info, sources, gathered(w_expand), *small, lambda i, t: t, True
        )
        spatial = [spatial]
        project_all = [gathered(w_project)]
        w_qkv, w_out = [gathered(w_qkv)], [gathered(w_out)]

    count = rows // CHUNKS
    rings = [list(range(first, space, groups)) for first in range(groups)]

    def exchange(parts):
        if len(parts) == 1:
            return [
                lax.all_to_all(parts[0], "space", 0, 0, axis_index_groups=rings, tiled=True)
            ]
        parts = list(parts)
        for k in ORDER:
            pairs_k = [
                (s, (((s // groups) ^ k) * groups) + s % groups) for s in range(space)
            ]
            parts[k] = lax.ppermute(parts[k], "space", pairs_k)
        return parts

    sent = [
        exchange(project_rows(info, spatial, ordered, project_all, chunk, count, SPLIT[chunk]))
        for chunk in range(CHUNKS)
    ]
    if pairs:
        w_qkv, w_out = [w_qkv, over_dp(w_qkv)], [w_out, over_dp(w_out)]
    back = [exchange(attend(info, parts, gain, bias, w_qkv, w_out)) for parts in sent]
    result = None
    for chunk in range(CHUNKS):
        result = restore_rows(info, back[chunk], rows, chunk, result)
    return result.reshape(fields.shape)


def solution(mesh):
    in_specs = (
        P("dp", "space", None, None),
        P(),
        P(),
        P(None, "dp"),
        P(),
        P(),
        P(),
        P(None, "dp"),
        P(),
        P(),
        P(None, "dp"),
        P(None, "dp"),
    )
    out_specs = P("dp", "space", None, None)
    return jax.shard_map(local, mesh=mesh, in_specs=in_specs, out_specs=out_specs, check_vma=False)
```

```python
import functools
import math

import jax
import jax.numpy as jnp
from jax import lax
from jax.experimental import pallas as pl
from jax.experimental.pallas import tpu as pltpu
from jax.sharding import PartitionSpec as P

HD = 32
GRID = 8
CHUNKS = 1
BATCH = 2
STRIPS = 2
SPLIT = (True,)
ORDER = (4, 6, 5, 7, 2, 3, 1)
ROOT = math.sqrt(2.0 / math.pi)
LIN = 2.0 * ROOT
CUBE = 8.0 * ROOT * 0.044715
F32 = jnp.float32
BF16 = jnp.bfloat16
VMEM_LIMIT = 18 * 1024 * 1024


def half_gelu(half):
    return half + half * jnp.tanh(half * (LIN + CUBE * (half * half)))


def one_hot_order(cols, inverse=False):
    stride = cols // GRID
    row = lax.broadcasted_iota(jnp.int32, (cols, cols), 0)
    col = lax.broadcasted_iota(jnp.int32, (cols, cols), 1)
    if inverse:
        row, col = col, row
    return jnp.where(col == (row % GRID) * stride + row // GRID, 1.0, 0.0).astype(BF16)


def dot(a, b):
    return jnp.dot(a, b, preferred_element_type=F32)


def vmem():
    return pl.BlockSpec(memory_space=pltpu.VMEM)


def smem():
    return pl.BlockSpec(memory_space=pltpu.SMEM)


def hbm():
    return pl.BlockSpec(memory_space=pltpu.HBM)


def in_hbm(array):
    return pltpu.with_memory_space_constraint(array, pltpu.HBM)


def any_space():
    return pl.BlockSpec(memory_space=pl.ANY)


def params():
    return pltpu.CompilerParams(vmem_limit_bytes=VMEM_LIMIT)


CORE, DP, SPACE, LAST, GROUPS = range(5)


def grid_of(info):
    return info[SPACE] // info[GROUPS]


def cost():
    return pl.CostEstimate(flops=1, bytes_accessed=1, transcendentals=1)


def copy_all(pairs, sems):
    copies = [pltpu.make_async_copy(src, dst, sems.at[n]) for n, (src, dst) in enumerate(pairs)]
    for copy in copies:
        copy.start()
    return copies


def edges_kernel(image, top, bottom, sems):
    rows = image.shape[0]
    for copy in copy_all([(image.at[rows - 1 : rows], bottom), (image.at[0:1], top)], sems):
        copy.wait()


def edge_rows(image):
    edge = jax.ShapeDtypeStruct((1,) + image.shape[1:], BF16)
    return pl.pallas_call(
        edges_kernel,
        in_specs=[hbm()],
        out_specs=[any_space()] * 2,
        out_shape=[edge, edge],
        scratch_shapes=[pltpu.SemaphoreType.DMA((2,))],
        compiler_params=params(),
        name="edge_rows",
    )(in_hbm(image))


def shares_kernel(info, expand, project, expand_part, project_part, sems):
    def span(part, axis):
        size = part.shape[axis]
        return pl.ds(pl.multiple_of(info[CORE] * size, size), size)

    moves = [
        (expand.at[:, span(expand_part, 1)], expand_part),
        (project.at[span(project_part, 0)], project_part),
    ]
    for copy in copy_all(moves, sems):
        copy.wait()


def share_weights(info, w_expand, w_project):
    shapes = [
        (w_expand.shape[0], w_expand.shape[1] // 2),
        (w_project.shape[0] // 2, w_project.shape[1]),
    ]
    return pl.pallas_call(
        shares_kernel,
        in_specs=[smem(), hbm(), hbm()],
        out_specs=[vmem()] * 2,
        out_shape=[jax.ShapeDtypeStruct(shape, BF16) for shape in shapes],
        scratch_shapes=[pltpu.SemaphoreType.DMA((2,))],
        compiler_params=params(),
        name="share_weights",
    )(info, *map(in_hbm, (w_expand, w_project)))


def order_kernel(image, above, below, scale, shift, ordered, normed):
    rows, cols, _ = image.shape
    pick = one_hot_order(cols)
    for row in range(rows + 2):
        if row == 0:
            placed = dot(pick, above[0])
        elif row == rows + 1:
            placed = dot(pick, below[0])
        else:
            placed = dot(pick, image[row - 1])
            ordered[row - 1] = placed.astype(BF16)
        normed[row] = (
            placed * (0.5 * scale[...]) + 0.5 * shift[...]
        ).astype(BF16)


def expand_kernel(first, tile_of, info, *refs):
    refs = list(refs)
    take = lambda n: [refs.pop(0) for _ in range(n)]
    step = pl.program_id(0)
    if first:
        image, above, below, scale, shift, weight, bias, taps, tap_bias = take(9)
        out, ordered, normed = take(3)
        raw, wide, sems, *held = refs
        moved = [(image, held[0])]
        moved += list(zip((scale, shift, weight, bias, taps, tap_bias), held[1:]))
        image, scale, shift, weight, bias, taps, tap_bias = held

        @pl.when(step == 0)
        def _():
            copies = copy_all(moved, sems)
            for copy in copies:
                copy.wait()
            order_kernel(image, above, below, scale, shift, ordered, normed)

    else:
        normed, weight, bias, taps, tap_bias, out, raw, wide = refs
    width = raw.shape[1]
    cols = wide.shape[1] - 2 * GRID
    rows = wide.shape[0] - 2
    if first:
        here = pl.ds(pl.multiple_of(step * width, width), width)
        tile = pl.ds(pl.multiple_of(tile_of(info, step) * width, width), width)
    else:
        here = tile = slice(None)
    weight = weight[:, here]
    half_bias = 0.5 * bias[:, tile]
    half_taps = 0.5 * taps[:, :, tile]
    half_tap_bias = 0.5 * tap_bias[:, tile]
    lane = lax.broadcasted_iota(jnp.int32, (GRID, width), 0)
    strip = cols // STRIPS
    blocks = [slice(lane, lane + 128) for lane in range(0, width, 128)]

    def product(row):
        tokens = normed[row : row + BATCH].reshape(BATCH * cols, -1)
        raw[row * cols : (row + BATCH) * cols, :] = dot(tokens, weight)

    def activate(row):
        value = half_gelu(raw[row * cols : (row + 1) * cols, :] + half_bias)
        if row == 0:
            value = value * jnp.where(info[SPACE] > 0, 1.0, 0.0)
        elif row == rows + 1:
            value = value * jnp.where(info[SPACE] < info[LAST], 1.0, 0.0)
        wide[row, GRID : GRID + cols, :] = value
        head = value[:GRID]
        tail = value[cols - GRID :]
        wide[row, :GRID, :] = jnp.where(lane == 0, 0.0, pltpu.roll(tail, 1, 0))
        wide[row, GRID + cols :, :] = jnp.where(
            lane == GRID - 1, 0.0, pltpu.roll(head, GRID - 1, 0)
        )

    def convolve(row):
        for lanes in blocks:
            for start in range(0, cols, strip):
                near = [
                    wide[row + off, start : start + strip + 2 * GRID, lanes] for off in range(3)
                ]
                total = half_tap_bias[:, lanes]
                for col_off in range(3):
                    for row_off in range(3):
                        part = near[row_off][GRID * col_off : GRID * col_off + strip]
                        total = total + part * half_taps[row_off, col_off, lanes][None]
                at = row * cols + start
                out[at : at + strip, lanes] = half_gelu(total).astype(BF16)

    product(0)
    for first_row in range(0, rows + 2, BATCH):
        if first_row + BATCH < rows + 2:
            product(first_row + BATCH)
        for row in range(first_row, first_row + BATCH):
            activate(row)
            if row >= 2:
                convolve(row - 2)


def expand_some(info, sources, weight, bias, taps, tap_bias, tile_of, first):
    chans, here = weight.shape
    width = min(256, here)
    if first:
        rows, cols, _ = sources[0].shape
    else:
        rows, cols = sources[0].shape[0] - 2, sources[0].shape[1]
    whole = lambda shape: pl.BlockSpec(shape, lambda t, info: (0,) * len(shape))
    held = []
    if first:
        in_specs = [hbm(), whole(sources[1].shape), whole(sources[2].shape)] + [hbm()] * 6
        fetched = [sources[0], *sources[3:], weight, bias, taps, tap_bias]
        held = [pltpu.SemaphoreType.DMA((len(fetched),))]
        held += [pltpu.VMEM(f.shape, f.dtype) for f in fetched]
    else:
        in_specs = [whole(s.shape) for s in sources]
        in_specs += [
            pl.BlockSpec((chans, width), lambda t, info: (0, t)),
            pl.BlockSpec((1, width), lambda t, info: (0, tile_of(info, t))),
            pl.BlockSpec((3, 3, width), lambda t, info: (0, 0, tile_of(info, t))),
            pl.BlockSpec((1, width), lambda t, info: (0, tile_of(info, t))),
        ]
    operands = [info, *sources, weight, bias, taps, tap_bias]
    if first:
        operands = [o if n in (0, 2, 3) else in_hbm(o) for n, o in enumerate(operands)]
    out_specs = [pl.BlockSpec((rows * cols, width), lambda t, info: (0, t))]
    out_shape = [jax.ShapeDtypeStruct((rows * cols, here), BF16)]
    if first:
        shapes = [(rows, cols, chans), (rows + 2, cols, chans)]
        out_specs += [whole(shape) for shape in shapes]
        out_shape += [jax.ShapeDtypeStruct(shape, BF16) for shape in shapes]
    return pl.pallas_call(
        functools.partial(expand_kernel, first, tile_of),
        grid_spec=pltpu.PrefetchScalarGridSpec(
            num_scalar_prefetch=1,
            grid=(here // width,),
            in_specs=in_specs,
            out_specs=out_specs,
            scratch_shapes=[
                pltpu.VMEM(((rows + 2) * cols, width), F32),
                pltpu.VMEM((rows + 2, cols + 2 * GRID, width), F32),
                *held,
            ],
        ),
        out_shape=out_shape,
        compiler_params=params(),
        cost_estimate=cost(),
        name="expand_conv",
    )(*operands)


def pieced_dot(lhs, pieces, info, put):
    width = pieces[0].shape[1]
    for n, piece in enumerate(pieces):
        if len(pieces) == 1:
            start = 0
        else:
            start = pl.multiple_of((1 - info[DP] if n else info[DP]) * width, width)
        put(start, width, dot(lhs[...], piece[...]))


def project_kernel(pieces, split, info, ordered, *refs):
    refs = list(refs)
    take = lambda n: [refs.pop(0) for _ in range(n)]
    spatial, weights, outs, (conv, other) = take(pieces), take(pieces), take(GRID if split else 1), refs
    count, cols, chans = ordered.shape
    size = cols // GRID
    own = weights[0]
    width = own.shape[1]

    def put(start, product):
        span = pl.ds(start, width)
        for row in range(count):
            at = slice(row * cols, (row + 1) * cols)
            conv[at, span] = (ordered[row, :, span].astype(F32) + product[at]).astype(BF16)

    if pieces == 1:
        put(0, dot(spatial[0][...], own[...]))
    else:
        mine, core = info[DP], info[CORE]
        half = own.shape[0] // 2
        for n, at in ((1, core), (2, 1 - core)):
            other[pl.ds(pl.multiple_of(at * half, half), half), :] = weights[n][...]
        part = half // 2
        starts = (
            (mine * half, half),
            ((1 - mine) * half + core * part, part),
            ((1 - mine) * half + (1 - core) * part, part),
        )
        for weight, column in ((own, mine), (other, 1 - mine)):
            total = None
            for lhs, (start, depth) in zip(spatial, starts):
                rows = pl.ds(pl.multiple_of(start, part), depth)
                product = dot(lhs[...], weight[rows, :])
                total = product if total is None else total + product
            put(pl.multiple_of(column * width, width), total)

    for k in range(GRID):
        place = (grid_of(info) ^ k) if split else k
        for row in range(count):
            start = row * cols + pl.multiple_of(place * size, size)
            block_of(outs, k)[row] = conv[pl.ds(start, size), :]


def block_of(parts, k):
    return parts[k] if len(parts) > 1 else parts[0].at[k]


def project_rows(info, spatial, ordered, weights, chunk, count, split):
    rows, cols, chans = ordered.shape
    size = cols // GRID
    block = (count, size, chans)
    outs = [block] * GRID if split else [(GRID,) + block]
    whole = lambda shape: pl.BlockSpec(shape, lambda t, info: (0,) * len(shape))
    return pl.pallas_call(
        functools.partial(project_kernel, len(weights), split),
        grid_spec=pltpu.PrefetchScalarGridSpec(
            num_scalar_prefetch=1,
            grid=(1,),
            in_specs=[pl.BlockSpec((count, cols, chans), lambda t, info: (chunk, 0, 0))]
            + [pl.BlockSpec((count * cols, s.shape[1]), lambda t, info: (chunk, 0)) for s in spatial]
            + [whole(w.shape) for w in weights],
            out_specs=[whole(out) for out in outs],
            scratch_shapes=[pltpu.VMEM((count * cols, chans), BF16), pltpu.VMEM(weights[0].shape, BF16)],
        ),
        out_shape=[jax.ShapeDtypeStruct(out, BF16) for out in outs],
        compiler_params=params(),
        cost_estimate=cost(),
        name="project_rows",
    )(info, ordered, *spatial, *weights)


def attend_kernel(pieces, blocks, info, gain, bias, *refs):
    refs = list(refs)
    take = lambda n: [refs.pop(0) for _ in range(n)]
    qkv_pieces, out_pieces = take(pieces), take(pieces)
    tokens, outs = take(blocks), take(blocks)
    lned, triple, mixed, resid, soft = refs
    count, size, chans = tokens[0].shape[-3:]
    wins = size // GRID
    length = GRID * GRID
    group = min(128, chans)
    heads = group // HD
    keys = heads * length

    for a in range(count):
        rows = [block_of(tokens, k)[a].astype(F32) for k in range(GRID)]
        for w in range(wins):
            x = jnp.concatenate([r[w * GRID : (w + 1) * GRID] for r in rows], axis=0)
            start = (a * wins + w) * length
            resid[start : start + length, :] = x
            center = jnp.mean(x, axis=-1, keepdims=True)
            off = x - center
            spread = jnp.mean(off * off, axis=-1, keepdims=True)
            lned[start : start + length, :] = (
                off * lax.rsqrt(spread + 1e-05) * gain[...] + bias[...]
            ).astype(BF16)

    def put_triple(start, width, product):
        triple[:, pl.ds(start, width)] = product.astype(BF16)

    pieced_dot(lned, qkv_pieces, info, put_triple)

    def same(shape, row_block, col_block):
        row = lax.broadcasted_iota(jnp.int32, shape, 0) // row_block
        col = lax.broadcasted_iota(jnp.int32, shape, 1) // col_block
        return jnp.where(row == col, 1.0, 0.0).astype(BF16)

    spread_mask = same((keys, group), length, HD)
    sum_mask = same((256, 256), length, length)
    factor = math.log2(math.e) / math.sqrt(HD)
    each = [(win, g) for win in range(count * wins) for g in range(chans // group)]
    spot = lambda win, g: (
        slice(win * length, (win + 1) * length),
        slice(g * keys, (g + 1) * keys),
    )
    for win, g in each:
        at, lanes = spot(win, g)
        query = triple[at, g * group : (g + 1) * group]
        key = triple[at, chans + g * group : chans + (g + 1) * group]
        key_wide = jnp.concatenate([key] * heads, axis=0) * spread_mask
        scores = lax.dot_general(
            query, key_wide, (((1,), (1,)), ((), ())), preferred_element_type=F32
        )
        soft[at, lanes] = jnp.minimum(jnp.exp2(scores * factor), 3.3895e38).astype(BF16)
    for start in range(0, count * wins * length, 256):
        for lane in range(0, soft.shape[1], 256):
            at, lanes = slice(start, start + 256), slice(lane, lane + 256)
            exponent = soft[at, lanes]
            soft[at, lanes] = (exponent.astype(F32) / dot(exponent, sum_mask)).astype(BF16)
    for win, g in each:
        at, lanes = spot(win, g)
        value = triple[at, 2 * chans + g * group : 2 * chans + (g + 1) * group]
        value_wide = jnp.concatenate([value] * heads, axis=0) * spread_mask
        mixed[at, g * group : (g + 1) * group] = dot(soft[at, lanes], value_wide).astype(BF16)

    def put_out(start, width, product):
        span = pl.ds(start, width)
        resid[:, span] = resid[:, span] + product

    pieced_dot(mixed, out_pieces, info, put_out)
    for a in range(count):
        for k in range(GRID):
            parts = []
            for w in range(wins):
                start = (a * wins + w) * length + k * GRID
                parts.append(resid[start : start + GRID, :])
            block_of(outs, k)[a] = jnp.concatenate(parts, axis=0).astype(BF16)


def attend(info, tokens, gain, bias, w_qkv, w_out):
    count, size, chans = tokens[0].shape[-3:]
    total = count * size * GRID
    return pl.pallas_call(
        functools.partial(attend_kernel, len(w_qkv), len(tokens)),
        out_shape=[jax.ShapeDtypeStruct(t.shape, BF16) for t in tokens],
        in_specs=[smem()] + [vmem()] * (2 + 2 * len(w_qkv) + len(tokens)),
        out_specs=[vmem()] * len(tokens),
        scratch_shapes=[
            pltpu.VMEM((total, chans), BF16),
            pltpu.VMEM((total, 3 * chans), BF16),
            pltpu.VMEM((total, chans), BF16),
            pltpu.VMEM((total, chans), F32),
            pltpu.VMEM((total, chans // HD * GRID * GRID), BF16),
        ],
        compiler_params=params(),
        cost_estimate=cost(),
        name="attend",
    )(info, gain, bias, *w_qkv, *w_out, *tokens)


def restore_kernel(blocks, info, *refs):
    parts = refs[:blocks]
    out, buf = refs[-2:]
    count, cols, chans = out.shape
    size = cols // GRID
    back = one_hot_order(cols, inverse=True)
    for row in range(count):
        if blocks == 1:
            tokens = parts[0][:, row].reshape(cols, chans)
        else:
            for k in range(GRID):
                place = pl.multiple_of((grid_of(info) ^ k) * size, size)
                buf[pl.ds(row * cols + place, size), :] = parts[k][row]
            tokens = buf[row * cols : (row + 1) * cols, :]
        out[row] = dot(back, tokens).astype(BF16)


def restore_rows(info, parts, rows, chunk, out):
    count, size, chans = parts[0].shape[-3:]
    cols = size * GRID
    in_specs = [pl.BlockSpec(p.shape, lambda t, i, n=p.ndim: (0,) * n) for p in parts]
    operands = [info, *parts]
    aliases = {}
    if out is not None:
        in_specs.append(pl.BlockSpec(memory_space=pl.ANY))
        aliases = {len(operands): 0}
        operands.append(out)
    return pl.pallas_call(
        functools.partial(restore_kernel, len(parts)),
        grid_spec=pltpu.PrefetchScalarGridSpec(
            num_scalar_prefetch=1,
            grid=(1,),
            in_specs=in_specs,
            out_specs=pl.BlockSpec((count, cols, chans), lambda t, info: (chunk, 0, 0)),
            scratch_shapes=[pltpu.VMEM((count * cols, chans), BF16)],
        ),
        out_shape=jax.ShapeDtypeStruct((rows, cols, chans), BF16),
        input_output_aliases=aliases,
        compiler_params=params(),
        cost_estimate=cost(),
        name="restore_rows",
    )(*operands)


def after(value, *others):
    return lax.optimization_barrier((value, *others))[0]


def local(
    fields,
    bn_scale,
    bn_shift,
    w_expand,
    expand_bias,
    dw_kernel,
    dw_bias,
    w_project,
    ln_gain,
    ln_bias,
    w_qkv,
    w_out,
):
    _, rows, cols, chans = fields.shape
    dp, space = lax.axis_size("dp"), lax.axis_size("space")
    dp_at, space_at = lax.axis_index("dp"), lax.axis_index("space")
    groups = space // GRID
    pairs = dp == 2 and space % 2 == 0
    info = jnp.stack(
        [
            jnp.asarray(v, jnp.int32)
            for v in (space_at % 2, dp_at, space_at, space - 1, groups)
        ]
    )
    as_row = lambda v: v.reshape(1, -1)
    image = fields.reshape(rows, cols, chans)
    small = (as_row(expand_bias), dw_kernel, as_row(dw_bias))
    gain, bias = as_row(ln_gain), as_row(ln_bias)

    over_dp = lambda w: lax.ppermute(w, "dp", [(0, 1), (1, 0)])
    over_core = lambda w: lax.ppermute(w, "space", [(i, i ^ 1) for i in range(space)])
    top, bottom = edge_rows(image)
    above = lax.ppermute(bottom, "space", [(i, i + 1) for i in range(space - 1)])
    below = lax.ppermute(top, "space", [(i + 1, i) for i in range(space - 1)])
    if pairs:
        mine = share_weights(after(info, top), w_expand, w_project)
        expand_got, project_got = map(over_dp, mine)
        above = after(above, *mine)
    sources = (image, above, below, as_row(bn_scale), as_row(bn_shift))
    if pairs:
        tiles = max(1, w_expand.shape[1] // 256)
        half = tiles // 2
        own_place = lambda i, t: i[DP] * tiles + t
        got_place = lambda i, t: (1 - i[DP]) * tiles + i[CORE] * half + t
        other_place = lambda i, t: (1 - i[DP]) * tiles + (1 - i[CORE]) * half + t
        own, ordered, normed = expand_some(info, sources, w_expand, *small, own_place, True)
        expand_got = after(expand_got, own)
        expand_other = over_core(expand_got)
        (got,) = expand_some(info, (normed,), expand_got, *small, got_place, False)
        expand_other, normed = lax.optimization_barrier((expand_other, normed, got))[:2]
        (other,) = expand_some(info, (normed,), expand_other, *small, other_place, False)
        spatial = [own, got, other]
        project_got = after(project_got, own)
        project_all = [w_project, project_got, over_core(project_got)]
    else:
        gathered = lambda w: lax.all_gather(w, "dp", axis=1, tiled=True)
        spatial, ordered, _ = expand_some(
            info, sources, gathered(w_expand), *small, lambda i, t: t, True
        )
        spatial = [spatial]
        project_all = [gathered(w_project)]
        w_qkv, w_out = [gathered(w_qkv)], [gathered(w_out)]

    count = rows // CHUNKS
    rings = [list(range(first, space, groups)) for first in range(groups)]

    def exchange(parts):
        if len(parts) == 1:
            return [
                lax.all_to_all(parts[0], "space", 0, 0, axis_index_groups=rings, tiled=True)
            ]
        parts = list(parts)
        for k in ORDER:
            pairs_k = [
                (s, (((s // groups) ^ k) * groups) + s % groups) for s in range(space)
            ]
            parts[k] = lax.ppermute(parts[k], "space", pairs_k)
        return parts

    sent = [
        exchange(project_rows(info, spatial, ordered, project_all, chunk, count, SPLIT[chunk]))
        for chunk in range(CHUNKS)
    ]
    if pairs:
        w_qkv, w_out = [w_qkv, over_dp(w_qkv)], [w_out, over_dp(w_out)]
    back = [exchange(attend(info, parts, gain, bias, w_qkv, w_out)) for parts in sent]
    result = None
    for chunk in range(CHUNKS):
        result = restore_rows(info, back[chunk], rows, chunk, result)
    return result.reshape(fields.shape)


def solution(mesh):
    in_specs = (
        P("dp", "space", None, None),
        P(),
        P(),
        P(None, "dp"),
        P(),
        P(),
        P(),
        P(None, "dp"),
        P(),
        P(),
        P(None, "dp"),
        P(None, "dp"),
    )
    out_specs = P("dp", "space", None, None)
    return jax.shard_map(local, mesh=mesh, in_specs=in_specs, out_specs=out_specs, check_vma=False)
```

```python
import functools
import math

import jax
import jax.numpy as jnp
from jax import lax
from jax.experimental import pallas as pl
from jax.experimental.pallas import tpu as pltpu
from jax.sharding import PartitionSpec as P

HD = 32
GRID = 8
BATCH = 2
STRIPS = 2
MOVES = (0, 1, 4, 6, 5, 2, 7, 3)
ROOT = math.sqrt(2.0 / math.pi)
LIN = 2.0 * ROOT
CUBE = 8.0 * ROOT * 0.044715
F32 = jnp.float32
BF16 = jnp.bfloat16
VMEM_LIMIT = 18 * 1024 * 1024


def half_gelu(half):
    return half + half * jnp.tanh(half * (LIN + CUBE * (half * half)))


def one_hot_order(cols, inverse=False):
    stride = cols // GRID
    row = lax.broadcasted_iota(jnp.int32, (cols, cols), 0)
    col = lax.broadcasted_iota(jnp.int32, (cols, cols), 1)
    if inverse:
        row, col = col, row
    return jnp.where(col == (row % GRID) * stride + row // GRID, 1.0, 0.0).astype(BF16)


def dot(a, b):
    return jnp.dot(a, b, preferred_element_type=F32)


def vmem():
    return pl.BlockSpec(memory_space=pltpu.VMEM)


def smem():
    return pl.BlockSpec(memory_space=pltpu.SMEM)


def hbm():
    return pl.BlockSpec(memory_space=pltpu.HBM)


def in_hbm(array):
    return pltpu.with_memory_space_constraint(array, pltpu.HBM)


def any_space():
    return pl.BlockSpec(memory_space=pl.ANY)


def params():
    return pltpu.CompilerParams(vmem_limit_bytes=VMEM_LIMIT)


CORE, DP, SPACE, LAST, GROUPS = range(5)


def grid_of(info):
    return info[SPACE] // info[GROUPS]


def cost():
    return pl.CostEstimate(flops=1, bytes_accessed=1, transcendentals=1)


def copy_all(pairs, sems):
    copies = [pltpu.make_async_copy(src, dst, sems.at[n]) for n, (src, dst) in enumerate(pairs)]
    for copy in copies:
        copy.start()
    return copies


def edges_kernel(info, image, top, bottom, sems):
    rows = image.shape[0]
    for copy in copy_all([(image.at[rows - 1 : rows], bottom), (image.at[0:1], top)], sems):
        copy.wait()


def edge_rows(info, image):
    edge = jax.ShapeDtypeStruct((1,) + image.shape[1:], BF16)
    return pl.pallas_call(
        edges_kernel,
        in_specs=[smem(), hbm()],
        out_specs=[vmem()] * 2,
        out_shape=[edge, edge],
        scratch_shapes=[pltpu.SemaphoreType.DMA((2,))],
        compiler_params=params(),
        name="edge_rows",
    )(info, in_hbm(image))


def shares_kernel(info, expand, project, qkv, out, expand_part, project_part, rest_part, sems):
    def span(part, axis):
        size = part.shape[axis]
        return pl.ds(pl.multiple_of(info[CORE] * size, size), size)

    width = qkv.shape[1]
    moves = [
        (expand.at[:, span(expand_part, 1)], expand_part),
        (project.at[span(project_part, 0)], project_part),
        (qkv.at[span(rest_part, 0)], rest_part.at[:, :width]),
        (out.at[span(rest_part, 0)], rest_part.at[:, width:]),
    ]
    for copy in copy_all(moves, sems):
        copy.wait()


def share_weights(info, w_expand, w_project, w_qkv, w_out):
    shapes = [
        (w_expand.shape[0], w_expand.shape[1] // 2),
        (w_project.shape[0] // 2, w_project.shape[1]),
        (w_qkv.shape[0] // 2, w_qkv.shape[1] + w_out.shape[1]),
    ]
    return pl.pallas_call(
        shares_kernel,
        in_specs=[smem()] + [hbm()] * 4,
        out_specs=[vmem()] * 3,
        out_shape=[jax.ShapeDtypeStruct(shape, BF16) for shape in shapes],
        scratch_shapes=[pltpu.SemaphoreType.DMA((4,))],
        compiler_params=params(),
        name="share_weights",
    )(info, *map(in_hbm, (w_expand, w_project, w_qkv, w_out)))


def order_kernel(image, above, below, scale, shift, ordered, normed):
    rows, cols, _ = image.shape
    pick = one_hot_order(cols)
    for row in range(rows + 2):
        if row == 0:
            placed = dot(pick, above[0])
        elif row == rows + 1:
            placed = dot(pick, below[0])
        else:
            placed = dot(pick, image[row - 1])
            ordered[row - 1] = placed.astype(BF16)
        normed[row] = (
            placed * (0.5 * scale[...]) + 0.5 * shift[...]
        ).astype(BF16)


def expand_kernel(first, tile_of, info, *refs):
    refs = list(refs)
    take = lambda n: [refs.pop(0) for _ in range(n)]
    step = pl.program_id(0)
    if first:
        image, above, below, scale, shift, weight, bias, taps, tap_bias = take(9)
        out, ordered, normed = take(3)
        raw, wide, sems, *held = refs
        moved = [(image, held[0])]
        moved += list(zip((scale, shift, weight, bias, taps, tap_bias), held[1:]))
        image, scale, shift, weight, bias, taps, tap_bias = held

        @pl.when(step == 0)
        def _():
            copies = copy_all(moved, sems)
            for copy in copies:
                copy.wait()
            order_kernel(image, above, below, scale, shift, ordered, normed)

    else:
        normed, weight, bias, taps, tap_bias, out, raw, wide = refs
    width = raw.shape[1]
    cols = wide.shape[1] - 2 * GRID
    rows = wide.shape[0] - 2
    if first:
        here = pl.ds(pl.multiple_of(step * width, width), width)
        tile = pl.ds(pl.multiple_of(tile_of(info, step) * width, width), width)
    else:
        here = tile = slice(None)
    weight = weight[:, here]
    half_bias = 0.5 * bias[:, tile]
    half_taps = 0.5 * taps[:, :, tile]
    half_tap_bias = 0.5 * tap_bias[:, tile]
    lane = lax.broadcasted_iota(jnp.int32, (GRID, width), 0)
    strip = cols // STRIPS
    blocks = [slice(lane, lane + 128) for lane in range(0, width, 128)]

    def product(row):
        tokens = normed[row : row + BATCH].reshape(BATCH * cols, -1)
        raw[row * cols : (row + BATCH) * cols, :] = dot(tokens, weight)

    def activate(row):
        value = half_gelu(raw[row * cols : (row + 1) * cols, :] + half_bias)
        if row == 0:
            value = value * jnp.where(info[SPACE] > 0, 1.0, 0.0)
        elif row == rows + 1:
            value = value * jnp.where(info[SPACE] < info[LAST], 1.0, 0.0)
        wide[row, GRID : GRID + cols, :] = value
        head = value[:GRID]
        tail = value[cols - GRID :]
        wide[row, :GRID, :] = jnp.where(lane == 0, 0.0, pltpu.roll(tail, 1, 0))
        wide[row, GRID + cols :, :] = jnp.where(
            lane == GRID - 1, 0.0, pltpu.roll(head, GRID - 1, 0)
        )

    def convolve(row):
        for lanes in blocks:
            for start in range(0, cols, strip):
                near = [
                    wide[row + off, start : start + strip + 2 * GRID, lanes] for off in range(3)
                ]
                total = half_tap_bias[:, lanes]
                for col_off in range(3):
                    for row_off in range(3):
                        part = near[row_off][GRID * col_off : GRID * col_off + strip]
                        total = total + part * half_taps[row_off, col_off, lanes][None]
                at = row * cols + start
                out[at : at + strip, lanes] = half_gelu(total).astype(BF16)

    product(0)
    for first_row in range(0, rows + 2, BATCH):
        if first_row + BATCH < rows + 2:
            product(first_row + BATCH)
        for row in range(first_row, first_row + BATCH):
            activate(row)
            if row >= 2:
                convolve(row - 2)


def expand_some(info, sources, weight, bias, taps, tap_bias, tile_of, first):
    chans, here = weight.shape
    width = min(256, here)
    if first:
        rows, cols, _ = sources[0].shape
    else:
        rows, cols = sources[0].shape[0] - 2, sources[0].shape[1]
    whole = lambda shape: pl.BlockSpec(shape, lambda t, info: (0,) * len(shape))
    held = []
    if first:
        in_specs = [hbm(), whole(sources[1].shape), whole(sources[2].shape)] + [hbm()] * 6
        fetched = [sources[0], *sources[3:], weight, bias, taps, tap_bias]
        held = [pltpu.SemaphoreType.DMA((len(fetched),))]
        held += [pltpu.VMEM(f.shape, f.dtype) for f in fetched]
    else:
        in_specs = [whole(s.shape) for s in sources]
        in_specs += [
            pl.BlockSpec((chans, width), lambda t, info: (0, t)),
            pl.BlockSpec((1, width), lambda t, info: (0, tile_of(info, t))),
            pl.BlockSpec((3, 3, width), lambda t, info: (0, 0, tile_of(info, t))),
            pl.BlockSpec((1, width), lambda t, info: (0, tile_of(info, t))),
        ]
    operands = [info, *sources, weight, bias, taps, tap_bias]
    if first:
        operands = [o if n in (0, 2, 3) else in_hbm(o) for n, o in enumerate(operands)]
    out_specs = [pl.BlockSpec((rows * cols, width), lambda t, info: (0, t))]
    out_shape = [jax.ShapeDtypeStruct((rows * cols, here), BF16)]
    if first:
        shapes = [(rows, cols, chans), (rows + 2, cols, chans)]
        out_specs += [whole(shape) for shape in shapes]
        out_shape += [jax.ShapeDtypeStruct(shape, BF16) for shape in shapes]
    return pl.pallas_call(
        functools.partial(expand_kernel, first, tile_of),
        grid_spec=pltpu.PrefetchScalarGridSpec(
            num_scalar_prefetch=1,
            grid=(here // width,),
            in_specs=in_specs,
            out_specs=out_specs,
            scratch_shapes=[
                pltpu.VMEM(((rows + 2) * cols, width), F32),
                pltpu.VMEM((rows + 2, cols + 2 * GRID, width), F32),
                *held,
            ],
        ),
        out_shape=out_shape,
        compiler_params=params(),
        cost_estimate=cost(),
        name="expand_conv",
    )(*operands)


def pieced_dot(lhs, pieces, info, put):
    width = pieces[0].shape[1]
    if len(pieces) == 1:
        put(0, width, dot(lhs[...], pieces[0][...]))
        return
    put(pl.multiple_of(info[DP] * width, width), width, dot(lhs[...], pieces[0][...]))
    total = None
    for n, piece in enumerate(pieces[1:]):
        depth = piece.shape[0]
        at = 1 - info[CORE] if n else info[CORE]
        part = dot(lhs[:, pl.ds(pl.multiple_of(at * depth, depth), depth)], piece[...])
        total = part if total is None else total + part
    put(pl.multiple_of((1 - info[DP]) * width, width), width, total)


def project_kernel(pieces, split, info, ordered, *refs):
    refs = list(refs)
    take = lambda n: [refs.pop(0) for _ in range(n)]
    spatial, weights, outs, (conv, other) = take(pieces), take(pieces), take(GRID if split else 1), refs
    count, cols, chans = ordered.shape
    size = cols // GRID
    own = weights[0]
    width = own.shape[1]

    def put(start, product):
        span = pl.ds(start, width)
        for row in range(count):
            at = slice(row * cols, (row + 1) * cols)
            conv[at, span] = (ordered[row, :, span].astype(F32) + product[at]).astype(BF16)

    if pieces == 1:
        put(0, dot(spatial[0][...], own[...]))
    else:
        mine, core = info[DP], info[CORE]
        half = own.shape[0] // 2
        for n, at in ((1, core), (2, 1 - core)):
            other[pl.ds(pl.multiple_of(at * half, half), half), :] = weights[n][...]
        part = half // 2
        starts = (
            (mine * half, half),
            ((1 - mine) * half + core * part, part),
            ((1 - mine) * half + (1 - core) * part, part),
        )
        for weight, column in ((own, mine), (other, 1 - mine)):
            total = None
            for lhs, (start, depth) in zip(spatial, starts):
                rows = pl.ds(pl.multiple_of(start, part), depth)
                product = dot(lhs[...], weight[rows, :])
                total = product if total is None else total + product
            put(pl.multiple_of(column * width, width), total)

    for k in range(GRID):
        place = (grid_of(info) ^ MOVES[k]) if split else k
        for row in range(count):
            start = row * cols + pl.multiple_of(place * size, size)
            block_of(outs, k)[row] = conv[pl.ds(start, size), :]


def block_of(parts, k):
    return parts[k] if len(parts) > 1 else parts[0].at[k]


def project_rows(info, spatial, ordered, weights, chunk, count, split):
    rows, cols, chans = ordered.shape
    size = cols // GRID
    block = (count, size, chans)
    outs = [block] * GRID if split else [(GRID,) + block]
    whole = lambda shape: pl.BlockSpec(shape, lambda t, info: (0,) * len(shape))
    return pl.pallas_call(
        functools.partial(project_kernel, len(weights), split),
        grid_spec=pltpu.PrefetchScalarGridSpec(
            num_scalar_prefetch=1,
            grid=(1,),
            in_specs=[pl.BlockSpec((count, cols, chans), lambda t, info: (chunk, 0, 0))]
            + [pl.BlockSpec((count * cols, s.shape[1]), lambda t, info: (chunk, 0)) for s in spatial]
            + [whole(w.shape) for w in weights],
            out_specs=[whole(out) for out in outs],
            scratch_shapes=[pltpu.VMEM((count * cols, chans), BF16), pltpu.VMEM(weights[0].shape, BF16)],
        ),
        out_shape=[jax.ShapeDtypeStruct(out, BF16) for out in outs],
        compiler_params=params(),
        cost_estimate=cost(),
        name="project_rows",
    )(info, ordered, *spatial, *weights)


def attend_kernel(pieces, blocks, info, gain, bias, *refs):
    refs = list(refs)
    take = lambda n: [refs.pop(0) for _ in range(n)]
    qkv_pieces, out_pieces, rest = take(1), take(1), take(pieces - 1)
    split = qkv_pieces[0].shape[1]
    for both in rest:
        qkv_pieces.append(both.at[:, :split])
        out_pieces.append(both.at[:, split:])
    tokens, outs = take(blocks), take(blocks)
    lned, triple, mixed, resid, soft = refs
    count, size, chans = tokens[0].shape[-3:]
    wins = size // GRID
    length = GRID * GRID
    group = min(128, chans)
    heads = group // HD
    keys = heads * length

    for a in range(count):
        rows = [block_of(tokens, k)[a].astype(F32) for k in range(GRID)]
        for w in range(wins):
            x = jnp.concatenate([r[w * GRID : (w + 1) * GRID] for r in rows], axis=0)
            start = (a * wins + w) * length
            resid[start : start + length, :] = x
            center = jnp.mean(x, axis=-1, keepdims=True)
            off = x - center
            spread = jnp.mean(off * off, axis=-1, keepdims=True)
            lned[start : start + length, :] = (
                off * lax.rsqrt(spread + 1e-05) * gain[...] + bias[...]
            ).astype(BF16)

    def put_triple(start, width, product):
        triple[:, pl.ds(start, width)] = product.astype(BF16)

    pieced_dot(lned, qkv_pieces, info, put_triple)

    def same(shape, row_block, col_block):
        row = lax.broadcasted_iota(jnp.int32, shape, 0) // row_block
        col = lax.broadcasted_iota(jnp.int32, shape, 1) // col_block
        return jnp.where(row == col, 1.0, 0.0).astype(BF16)

    spread_mask = same((keys, group), length, HD)
    sum_mask = same((256, 256), length, length)
    factor = math.log2(math.e) / math.sqrt(HD)
    each = [(win, g) for win in range(count * wins) for g in range(chans // group)]
    spot = lambda win, g: (
        slice(win * length, (win + 1) * length),
        slice(g * keys, (g + 1) * keys),
    )
    for win, g in each:
        at, lanes = spot(win, g)
        query = triple[at, g * group : (g + 1) * group]
        key = triple[at, chans + g * group : chans + (g + 1) * group]
        key_wide = jnp.concatenate([key] * heads, axis=0) * spread_mask
        scores = lax.dot_general(
            query, key_wide, (((1,), (1,)), ((), ())), preferred_element_type=F32
        )
        soft[at, lanes] = jnp.minimum(jnp.exp2(scores * factor), 3.3895e38).astype(BF16)
    for start in range(0, count * wins * length, 256):
        for lane in range(0, soft.shape[1], 256):
            at, lanes = slice(start, start + 256), slice(lane, lane + 256)
            exponent = soft[at, lanes]
            soft[at, lanes] = (exponent.astype(F32) / dot(exponent, sum_mask)).astype(BF16)
    for win, g in each:
        at, lanes = spot(win, g)
        value = triple[at, 2 * chans + g * group : 2 * chans + (g + 1) * group]
        value_wide = jnp.concatenate([value] * heads, axis=0) * spread_mask
        mixed[at, g * group : (g + 1) * group] = dot(soft[at, lanes], value_wide).astype(BF16)

    def put_out(start, width, product):
        span = pl.ds(start, width)
        resid[:, span] = resid[:, span] + product

    pieced_dot(mixed, out_pieces, info, put_out)
    for a in range(count):
        for k in range(GRID):
            parts = []
            for w in range(wins):
                start = (a * wins + w) * length + k * GRID
                parts.append(resid[start : start + GRID, :])
            block_of(outs, k)[a] = jnp.concatenate(parts, axis=0).astype(BF16)


def attend(info, tokens, gain, bias, w_qkv, w_out, rest):
    count, size, chans = tokens[0].shape[-3:]
    total = count * size * GRID
    return pl.pallas_call(
        functools.partial(attend_kernel, 1 + len(rest), len(tokens)),
        out_shape=[jax.ShapeDtypeStruct(t.shape, BF16) for t in tokens],
        in_specs=[smem()] + [vmem()] * (4 + len(rest) + len(tokens)),
        out_specs=[vmem()] * len(tokens),
        scratch_shapes=[
            pltpu.VMEM((total, chans), BF16),
            pltpu.VMEM((total, 3 * chans), BF16),
            pltpu.VMEM((total, chans), BF16),
            pltpu.VMEM((total, chans), F32),
            pltpu.VMEM((total, chans // HD * GRID * GRID), BF16),
        ],
        compiler_params=params(),
        cost_estimate=cost(),
        name="attend",
    )(info, gain, bias, w_qkv, w_out, *rest, *tokens)


def restore_kernel(blocks, info, *refs):
    parts = refs[:blocks]
    out, buf = refs[-2:]
    count, cols, chans = out.shape
    size = cols // GRID
    back = one_hot_order(cols, inverse=True)
    for row in range(count):
        if blocks == 1:
            tokens = parts[0][:, row].reshape(cols, chans)
        else:
            for k in range(GRID):
                place = pl.multiple_of((grid_of(info) ^ MOVES[k]) * size, size)
                buf[pl.ds(row * cols + place, size), :] = parts[k][row]
            tokens = buf[row * cols : (row + 1) * cols, :]
        out[row] = dot(back, tokens).astype(BF16)


def restore_rows(info, parts, rows, chunk, out):
    count, size, chans = parts[0].shape[-3:]
    cols = size * GRID
    in_specs = [pl.BlockSpec(p.shape, lambda t, i, n=p.ndim: (0,) * n) for p in parts]
    operands = [info, *parts]
    aliases = {}
    if out is not None:
        in_specs.append(pl.BlockSpec(memory_space=pl.ANY))
        aliases = {len(operands): 0}
        operands.append(out)
    return pl.pallas_call(
        functools.partial(restore_kernel, len(parts)),
        grid_spec=pltpu.PrefetchScalarGridSpec(
            num_scalar_prefetch=1,
            grid=(1,),
            in_specs=in_specs,
            out_specs=pl.BlockSpec((count, cols, chans), lambda t, info: (chunk, 0, 0)),
            scratch_shapes=[pltpu.VMEM((count * cols, chans), BF16)],
        ),
        out_shape=jax.ShapeDtypeStruct((rows, cols, chans), BF16),
        input_output_aliases=aliases,
        compiler_params=params(),
        cost_estimate=cost(),
        name="restore_rows",
    )(*operands)


def after(value, *others):
    return lax.optimization_barrier((value, *others))[0]


def local(
    fields,
    bn_scale,
    bn_shift,
    w_expand,
    expand_bias,
    dw_kernel,
    dw_bias,
    w_project,
    ln_gain,
    ln_bias,
    w_qkv,
    w_out,
):
    _, rows, cols, chans = fields.shape
    dp, space = lax.axis_size("dp"), lax.axis_size("space")
    dp_at, space_at = lax.axis_index("dp"), lax.axis_index("space")
    groups = space // GRID
    pairs = dp == 2 and space % 2 == 0
    info = jnp.stack(
        [
            jnp.asarray(v, jnp.int32)
            for v in (space_at % 2, dp_at, space_at, space - 1, groups)
        ]
    )
    as_row = lambda v: v.reshape(1, -1)
    image = fields.reshape(rows, cols, chans)
    small = (as_row(expand_bias), dw_kernel, as_row(dw_bias))
    gain, bias = as_row(ln_gain), as_row(ln_bias)

    over_dp = lambda w: lax.ppermute(w, "dp", [(0, 1), (1, 0)])
    over_core = lambda w: lax.ppermute(w, "space", [(i, i ^ 1) for i in range(space)])
    later = info
    if pairs:
        mine = share_weights(info, w_expand, w_project, w_qkv, w_out)
        expand_got, project_got, rest_got = map(over_dp, mine)
        later = after(info, *mine)
    top, bottom = edge_rows(later, image)
    above = lax.ppermute(bottom, "space", [(i, (i + 1) % space) for i in range(space)])
    below = lax.ppermute(top, "space", [((i + 1) % space, i) for i in range(space)])
    sources = (image, above, below, as_row(bn_scale), as_row(bn_shift))
    if pairs:
        tiles = max(1, w_expand.shape[1] // 256)
        half = tiles // 2
        own_place = lambda i, t: i[DP] * tiles + t
        got_place = lambda i, t: (1 - i[DP]) * tiles + i[CORE] * half + t
        other_place = lambda i, t: (1 - i[DP]) * tiles + (1 - i[CORE]) * half + t
        own, ordered, normed = expand_some(info, sources, w_expand, *small, own_place, True)
        expand_got = after(expand_got, own)
        expand_other = over_core(expand_got)
        (got,) = expand_some(info, (normed,), expand_got, *small, got_place, False)
        expand_other, normed = lax.optimization_barrier((expand_other, normed, got))[:2]
        (other,) = expand_some(info, (normed,), expand_other, *small, other_place, False)
        spatial = [own, got, other]
        project_got = after(project_got, own)
        project_all = [w_project, project_got, over_core(project_got)]
    else:
        gathered = lambda w: lax.all_gather(w, "dp", axis=1, tiled=True)
        spatial, ordered, _ = expand_some(
            info, sources, gathered(w_expand), *small, lambda i, t: t, True
        )
        spatial = [spatial]
        project_all = [gathered(w_project)]
        w_qkv, w_out = gathered(w_qkv), gathered(w_out)


    def exchange(parts):
        parts = list(parts)
        for n in range(1, GRID):
            swap = [
                (s, (((s // groups) ^ MOVES[n]) * groups) + s % groups) for s in range(space)
            ]
            parts[n] = lax.ppermute(parts[n], "space", swap)
        return parts

    placed = project_rows(info, spatial, ordered, project_all, 0, rows, True)
    rest = []
    if pairs:
        rest_got = after(rest_got, placed[0])
        rest = [rest_got, over_core(rest_got)]
    back = exchange(attend(info, exchange(placed), gain, bias, w_qkv, w_out, rest))
    result = restore_rows(info, back, rows, 0, None)
    return result.reshape(fields.shape)


def solution(mesh):
    in_specs = (
        P("dp", "space", None, None),
        P(),
        P(),
        P(None, "dp"),
        P(),
        P(),
        P(),
        P(None, "dp"),
        P(),
        P(),
        P(None, "dp"),
        P(None, "dp"),
    )
    out_specs = P("dp", "space", None, None)
    return jax.shard_map(local, mesh=mesh, in_specs=in_specs, out_specs=out_specs, check_vma=False)
```

```python
import functools
import math

import jax
import jax.numpy as jnp
from jax import lax
from jax.experimental import pallas as pl
from jax.experimental.pallas import tpu as pltpu
from jax.sharding import PartitionSpec as P

HD = 32
GRID = 8
BATCH = 2
STRIPS = 2
MOVES = (0, 1, 4, 6, 5, 2, 7, 3)
ROOT = math.sqrt(2.0 / math.pi)
LIN = 2.0 * ROOT
CUBE = 8.0 * ROOT * 0.044715
F32 = jnp.float32
BF16 = jnp.bfloat16
VMEM_LIMIT = 18 * 1024 * 1024


def half_gelu(half):
    return half + half * jnp.tanh(half * (LIN + CUBE * (half * half)))


def one_hot_order(cols, inverse=False):
    stride = cols // GRID
    row = lax.broadcasted_iota(jnp.int32, (cols, cols), 0)
    col = lax.broadcasted_iota(jnp.int32, (cols, cols), 1)
    if inverse:
        row, col = col, row
    return jnp.where(col == (row % GRID) * stride + row // GRID, 1.0, 0.0).astype(BF16)


def dot(a, b):
    return jnp.dot(a, b, preferred_element_type=F32)


def vmem():
    return pl.BlockSpec(memory_space=pltpu.VMEM)


def smem():
    return pl.BlockSpec(memory_space=pltpu.SMEM)


def hbm():
    return pl.BlockSpec(memory_space=pltpu.HBM)


def in_hbm(array):
    return pltpu.with_memory_space_constraint(array, pltpu.HBM)


def any_space():
    return pl.BlockSpec(memory_space=pl.ANY)


def params():
    return pltpu.CompilerParams(vmem_limit_bytes=VMEM_LIMIT)


CORE, DP, SPACE, LAST, GROUPS = range(5)


def grid_of(info):
    return info[SPACE] // info[GROUPS]


def cost():
    return pl.CostEstimate(flops=1, bytes_accessed=1, transcendentals=1)


def copy_all(pairs, sems):
    copies = [pltpu.make_async_copy(src, dst, sems.at[n]) for n, (src, dst) in enumerate(pairs)]
    for copy in copies:
        copy.start()
    return copies


def edges_kernel(info, image, top, bottom, sems):
    rows = image.shape[0]
    for copy in copy_all([(image.at[rows - 1 : rows], bottom), (image.at[0:1], top)], sems):
        copy.wait()


def edge_rows(info, image):
    edge = jax.ShapeDtypeStruct((1,) + image.shape[1:], BF16)
    return pl.pallas_call(
        edges_kernel,
        in_specs=[smem(), hbm()],
        out_specs=[vmem()] * 2,
        out_shape=[edge, edge],
        scratch_shapes=[pltpu.SemaphoreType.DMA((2,))],
        compiler_params=params(),
        name="edge_rows",
    )(info, in_hbm(image))


def share_of(info, part, axis):
    size = part.shape[axis]
    return pl.ds(pl.multiple_of(info[CORE] * size, size), size)


def expand_share_kernel(info, expand, part, sems):
    for copy in copy_all([(expand.at[:, share_of(info, part, 1)], part)], sems):
        copy.wait()


def shares_kernel(info, project, qkv, out, project_part, rest_part, sems):
    width = qkv.shape[1]
    moves = [
        (project.at[share_of(info, project_part, 0)], project_part),
        (qkv.at[share_of(info, rest_part, 0)], rest_part.at[:, :width]),
        (out.at[share_of(info, rest_part, 0)], rest_part.at[:, width:]),
    ]
    for copy in copy_all(moves, sems):
        copy.wait()


def share_weights(kernel, info, weights, shapes, name):
    return pl.pallas_call(
        kernel,
        in_specs=[smem()] + [hbm()] * len(weights),
        out_specs=[vmem()] * len(shapes),
        out_shape=[jax.ShapeDtypeStruct(shape, BF16) for shape in shapes],
        scratch_shapes=[pltpu.SemaphoreType.DMA((len(weights),))],
        compiler_params=params(),
        name=name,
    )(info, *map(in_hbm, weights))


def order_kernel(image, above, below, scale, shift, ordered, normed):
    rows, cols, _ = image.shape
    pick = one_hot_order(cols)
    for row in range(rows + 2):
        if row == 0:
            placed = dot(pick, above[0])
        elif row == rows + 1:
            placed = dot(pick, below[0])
        else:
            placed = dot(pick, image[row - 1])
            ordered[row - 1] = placed.astype(BF16)
        normed[row] = (
            placed * (0.5 * scale[...]) + 0.5 * shift[...]
        ).astype(BF16)


def expand_kernel(first, tile_of, info, *refs):
    refs = list(refs)
    take = lambda n: [refs.pop(0) for _ in range(n)]
    step = pl.program_id(0)
    if first:
        image, above, below, scale, shift, weight, bias, taps, tap_bias = take(9)
        out, ordered, normed = take(3)
        raw, wide, sems, *held = refs
        moved = [(image, held[0])]
        moved += list(zip((scale, shift, weight, bias, taps, tap_bias), held[1:]))
        image, scale, shift, weight, bias, taps, tap_bias = held

        @pl.when(step == 0)
        def _():
            copies = copy_all(moved, sems)
            for copy in copies:
                copy.wait()
            order_kernel(image, above, below, scale, shift, ordered, normed)

    else:
        normed, weight, bias, taps, tap_bias, out, raw, wide = refs
    width = raw.shape[1]
    cols = wide.shape[1] - 2 * GRID
    rows = wide.shape[0] - 2
    if first:
        here = pl.ds(pl.multiple_of(step * width, width), width)
        tile = pl.ds(pl.multiple_of(tile_of(info, step) * width, width), width)
    else:
        here = tile = slice(None)
    weight = weight[:, here]
    half_bias = 0.5 * bias[:, tile]
    half_taps = 0.5 * taps[:, :, tile]
    half_tap_bias = 0.5 * tap_bias[:, tile]
    lane = lax.broadcasted_iota(jnp.int32, (GRID, width), 0)
    strip = cols // STRIPS
    blocks = [slice(lane, lane + 128) for lane in range(0, width, 128)]

    def product(row):
        tokens = normed[row : row + BATCH].reshape(BATCH * cols, -1)
        raw[row * cols : (row + BATCH) * cols, :] = dot(tokens, weight)

    def activate(row):
        value = half_gelu(raw[row * cols : (row + 1) * cols, :] + half_bias)
        if row == 0:
            value = value * jnp.where(info[SPACE] > 0, 1.0, 0.0)
        elif row == rows + 1:
            value = value * jnp.where(info[SPACE] < info[LAST], 1.0, 0.0)
        wide[row, GRID : GRID + cols, :] = value
        head = value[:GRID]
        tail = value[cols - GRID :]
        wide[row, :GRID, :] = jnp.where(lane == 0, 0.0, pltpu.roll(tail, 1, 0))
        wide[row, GRID + cols :, :] = jnp.where(
            lane == GRID - 1, 0.0, pltpu.roll(head, GRID - 1, 0)
        )

    def convolve(row):
        for lanes in blocks:
            for start in range(0, cols, strip):
                near = [
                    wide[row + off, start : start + strip + 2 * GRID, lanes] for off in range(3)
                ]
                total = half_tap_bias[:, lanes]
                for col_off in range(3):
                    for row_off in range(3):
                        part = near[row_off][GRID * col_off : GRID * col_off + strip]
                        total = total + part * half_taps[row_off, col_off, lanes][None]
                at = row * cols + start
                out[at : at + strip, lanes] = half_gelu(total).astype(BF16)

    product(0)
    for first_row in range(0, rows + 2, BATCH):
        if first_row + BATCH < rows + 2:
            product(first_row + BATCH)
        for row in range(first_row, first_row + BATCH):
            activate(row)
            if row >= 2:
                convolve(row - 2)


def expand_some(info, sources, weight, bias, taps, tap_bias, tile_of, first):
    chans, here = weight.shape
    width = min(256, here)
    if first:
        rows, cols, _ = sources[0].shape
    else:
        rows, cols = sources[0].shape[0] - 2, sources[0].shape[1]
    whole = lambda shape: pl.BlockSpec(shape, lambda t, info: (0,) * len(shape))
    held = []
    if first:
        in_specs = [hbm(), whole(sources[1].shape), whole(sources[2].shape)] + [hbm()] * 6
        fetched = [sources[0], *sources[3:], weight, bias, taps, tap_bias]
        held = [pltpu.SemaphoreType.DMA((len(fetched),))]
        held += [pltpu.VMEM(f.shape, f.dtype) for f in fetched]
    else:
        in_specs = [whole(s.shape) for s in sources]
        in_specs += [
            pl.BlockSpec((chans, width), lambda t, info: (0, t)),
            pl.BlockSpec((1, width), lambda t, info: (0, tile_of(info, t))),
            pl.BlockSpec((3, 3, width), lambda t, info: (0, 0, tile_of(info, t))),
            pl.BlockSpec((1, width), lambda t, info: (0, tile_of(info, t))),
        ]
    operands = [info, *sources, weight, bias, taps, tap_bias]
    if first:
        operands = [o if n in (0, 2, 3) else in_hbm(o) for n, o in enumerate(operands)]
    out_specs = [pl.BlockSpec((rows * cols, width), lambda t, info: (0, t))]
    out_shape = [jax.ShapeDtypeStruct((rows * cols, here), BF16)]
    if first:
        shapes = [(rows, cols, chans), (rows + 2, cols, chans)]
        out_specs += [whole(shape) for shape in shapes]
        out_shape += [jax.ShapeDtypeStruct(shape, BF16) for shape in shapes]
    return pl.pallas_call(
        functools.partial(expand_kernel, first, tile_of),
        grid_spec=pltpu.PrefetchScalarGridSpec(
            num_scalar_prefetch=1,
            grid=(here // width,),
            in_specs=in_specs,
            out_specs=out_specs,
            scratch_shapes=[
                pltpu.VMEM(((rows + 2) * cols, width), F32),
                pltpu.VMEM((rows + 2, cols + 2 * GRID, width), F32),
                *held,
            ],
        ),
        out_shape=out_shape,
        compiler_params=params(),
        cost_estimate=cost(),
        name="expand_conv",
    )(*operands)


def pieced_dot(lhs, pieces, info, put):
    width = pieces[0].shape[1]
    if len(pieces) == 1:
        put(0, width, dot(lhs[...], pieces[0][...]))
        return
    put(pl.multiple_of(info[DP] * width, width), width, dot(lhs[...], pieces[0][...]))
    total = None
    for n, piece in enumerate(pieces[1:]):
        depth = piece.shape[0]
        at = 1 - info[CORE] if n else info[CORE]
        part = dot(lhs[:, pl.ds(pl.multiple_of(at * depth, depth), depth)], piece[...])
        total = part if total is None else total + part
    put(pl.multiple_of((1 - info[DP]) * width, width), width, total)


def project_kernel(pieces, split, info, ordered, *refs):
    refs = list(refs)
    take = lambda n: [refs.pop(0) for _ in range(n)]
    spatial, weights, outs, (conv, other) = take(pieces), take(pieces), take(GRID if split else 1), refs
    count, cols, chans = ordered.shape
    size = cols // GRID
    own = weights[0]
    width = own.shape[1]

    def put(start, product):
        span = pl.ds(start, width)
        for row in range(count):
            at = slice(row * cols, (row + 1) * cols)
            conv[at, span] = (ordered[row, :, span].astype(F32) + product[at]).astype(BF16)

    if pieces == 1:
        put(0, dot(spatial[0][...], own[...]))
    else:
        mine, core = info[DP], info[CORE]
        half = own.shape[0] // 2
        for n, at in ((1, core), (2, 1 - core)):
            other[pl.ds(pl.multiple_of(at * half, half), half), :] = weights[n][...]
        part = half // 2
        starts = (
            (mine * half, half),
            ((1 - mine) * half + core * part, part),
            ((1 - mine) * half + (1 - core) * part, part),
        )
        for weight, column in ((own, mine), (other, 1 - mine)):
            total = None
            for lhs, (start, depth) in zip(spatial, starts):
                rows = pl.ds(pl.multiple_of(start, part), depth)
                product = dot(lhs[...], weight[rows, :])
                total = product if total is None else total + product
            put(pl.multiple_of(column * width, width), total)

    for k in range(GRID):
        place = (grid_of(info) ^ MOVES[k]) if split else k
        for row in range(count):
            start = row * cols + pl.multiple_of(place * size, size)
            block_of(outs, k)[row] = conv[pl.ds(start, size), :]


def block_of(parts, k):
    return parts[k] if len(parts) > 1 else parts[0].at[k]


def project_rows(info, spatial, ordered, weights, chunk, count, split):
    rows, cols, chans = ordered.shape
    size = cols // GRID
    block = (count, size, chans)
    outs = [block] * GRID if split else [(GRID,) + block]
    whole = lambda shape: pl.BlockSpec(shape, lambda t, info: (0,) * len(shape))
    return pl.pallas_call(
        functools.partial(project_kernel, len(weights), split),
        grid_spec=pltpu.PrefetchScalarGridSpec(
            num_scalar_prefetch=1,
            grid=(1,),
            in_specs=[pl.BlockSpec((count, cols, chans), lambda t, info: (chunk, 0, 0))]
            + [pl.BlockSpec((count * cols, s.shape[1]), lambda t, info: (chunk, 0)) for s in spatial]
            + [whole(w.shape) for w in weights],
            out_specs=[whole(out) for out in outs],
            scratch_shapes=[pltpu.VMEM((count * cols, chans), BF16), pltpu.VMEM(weights[0].shape, BF16)],
        ),
        out_shape=[jax.ShapeDtypeStruct(out, BF16) for out in outs],
        compiler_params=params(),
        cost_estimate=cost(),
        name="project_rows",
    )(info, ordered, *spatial, *weights)


def attend_kernel(pieces, blocks, info, gain, bias, *refs):
    refs = list(refs)
    take = lambda n: [refs.pop(0) for _ in range(n)]
    qkv_pieces, out_pieces, rest = take(1), take(1), take(pieces - 1)
    split = qkv_pieces[0].shape[1]
    for both in rest:
        qkv_pieces.append(both.at[:, :split])
        out_pieces.append(both.at[:, split:])
    tokens, outs = take(blocks), take(blocks)
    lned, triple, mixed, resid, soft = refs
    count, size, chans = tokens[0].shape[-3:]
    wins = size // GRID
    length = GRID * GRID
    group = min(128, chans)
    heads = group // HD
    keys = heads * length

    for a in range(count):
        rows = [block_of(tokens, k)[a].astype(F32) for k in range(GRID)]
        for w in range(wins):
            x = jnp.concatenate([r[w * GRID : (w + 1) * GRID] for r in rows], axis=0)
            start = (a * wins + w) * length
            resid[start : start + length, :] = x
            center = jnp.mean(x, axis=-1, keepdims=True)
            off = x - center
            spread = jnp.mean(off * off, axis=-1, keepdims=True)
            lned[start : start + length, :] = (
                off * lax.rsqrt(spread + 1e-05) * gain[...] + bias[...]
            ).astype(BF16)

    def put_triple(start, width, product):
        triple[:, pl.ds(start, width)] = product.astype(BF16)

    pieced_dot(lned, qkv_pieces, info, put_triple)

    def same(shape, row_block, col_block):
        row = lax.broadcasted_iota(jnp.int32, shape, 0) // row_block
        col = lax.broadcasted_iota(jnp.int32, shape, 1) // col_block
        return jnp.where(row == col, 1.0, 0.0).astype(BF16)

    spread_mask = same((keys, group), length, HD)
    sum_mask = same((256, 256), length, length)
    factor = math.log2(math.e) / math.sqrt(HD)
    each = [(win, g) for win in range(count * wins) for g in range(chans // group)]
    spot = lambda win, g: (
        slice(win * length, (win + 1) * length),
        slice(g * keys, (g + 1) * keys),
    )
    for win, g in each:
        at, lanes = spot(win, g)
        query = triple[at, g * group : (g + 1) * group]
        key = triple[at, chans + g * group : chans + (g + 1) * group]
        key_wide = jnp.concatenate([key] * heads, axis=0) * spread_mask
        scores = lax.dot_general(
            query, key_wide, (((1,), (1,)), ((), ())), preferred_element_type=F32
        )
        soft[at, lanes] = jnp.minimum(jnp.exp2(scores * factor), 3.3895e38).astype(BF16)
    for start in range(0, count * wins * length, 256):
        for lane in range(0, soft.shape[1], 256):
            at, lanes = slice(start, start + 256), slice(lane, lane + 256)
            exponent = soft[at, lanes]
            soft[at, lanes] = (exponent.astype(F32) / dot(exponent, sum_mask)).astype(BF16)
    for win, g in each:
        at, lanes = spot(win, g)
        value = triple[at, 2 * chans + g * group : 2 * chans + (g + 1) * group]
        value_wide = jnp.concatenate([value] * heads, axis=0) * spread_mask
        mixed[at, g * group : (g + 1) * group] = dot(soft[at, lanes], value_wide).astype(BF16)

    def put_out(start, width, product):
        span = pl.ds(start, width)
        resid[:, span] = resid[:, span] + product

    pieced_dot(mixed, out_pieces, info, put_out)
    for a in range(count):
        for k in range(GRID):
            parts = []
            for w in range(wins):
                start = (a * wins + w) * length + k * GRID
                parts.append(resid[start : start + GRID, :])
            block_of(outs, k)[a] = jnp.concatenate(parts, axis=0).astype(BF16)


def attend(info, tokens, gain, bias, w_qkv, w_out, rest):
    count, size, chans = tokens[0].shape[-3:]
    total = count * size * GRID
    return pl.pallas_call(
        functools.partial(attend_kernel, 1 + len(rest), len(tokens)),
        out_shape=[jax.ShapeDtypeStruct(t.shape, BF16) for t in tokens],
        in_specs=[smem()] + [vmem()] * (4 + len(rest) + len(tokens)),
        out_specs=[vmem()] * len(tokens),
        scratch_shapes=[
            pltpu.VMEM((total, chans), BF16),
            pltpu.VMEM((total, 3 * chans), BF16),
            pltpu.VMEM((total, chans), BF16),
            pltpu.VMEM((total, chans), F32),
            pltpu.VMEM((total, chans // HD * GRID * GRID), BF16),
        ],
        compiler_params=params(),
        cost_estimate=cost(),
        name="attend",
    )(info, gain, bias, w_qkv, w_out, *rest, *tokens)


def restore_kernel(blocks, info, *refs):
    parts = refs[:blocks]
    out, buf = refs[-2:]
    count, cols, chans = out.shape
    size = cols // GRID
    back = one_hot_order(cols, inverse=True)
    for row in range(count):
        if blocks == 1:
            tokens = parts[0][:, row].reshape(cols, chans)
        else:
            for k in range(GRID):
                place = pl.multiple_of((grid_of(info) ^ MOVES[k]) * size, size)
                buf[pl.ds(row * cols + place, size), :] = parts[k][row]
            tokens = buf[row * cols : (row + 1) * cols, :]
        out[row] = dot(back, tokens).astype(BF16)


def restore_rows(info, parts, rows, chunk, out):
    count, size, chans = parts[0].shape[-3:]
    cols = size * GRID
    in_specs = [pl.BlockSpec(p.shape, lambda t, i, n=p.ndim: (0,) * n) for p in parts]
    operands = [info, *parts]
    aliases = {}
    if out is not None:
        in_specs.append(pl.BlockSpec(memory_space=pl.ANY))
        aliases = {len(operands): 0}
        operands.append(out)
    return pl.pallas_call(
        functools.partial(restore_kernel, len(parts)),
        grid_spec=pltpu.PrefetchScalarGridSpec(
            num_scalar_prefetch=1,
            grid=(1,),
            in_specs=in_specs,
            out_specs=pl.BlockSpec((count, cols, chans), lambda t, info: (chunk, 0, 0)),
            scratch_shapes=[pltpu.VMEM((count * cols, chans), BF16)],
        ),
        out_shape=jax.ShapeDtypeStruct((rows, cols, chans), BF16),
        input_output_aliases=aliases,
        compiler_params=params(),
        cost_estimate=cost(),
        name="restore_rows",
    )(*operands)


def after(value, *others):
    return lax.optimization_barrier((value, *others))[0]


def local(
    fields,
    bn_scale,
    bn_shift,
    w_expand,
    expand_bias,
    dw_kernel,
    dw_bias,
    w_project,
    ln_gain,
    ln_bias,
    w_qkv,
    w_out,
):
    _, rows, cols, chans = fields.shape
    dp, space = lax.axis_size("dp"), lax.axis_size("space")
    dp_at, space_at = lax.axis_index("dp"), lax.axis_index("space")
    groups = space // GRID
    pairs = dp == 2 and space % 2 == 0
    info = jnp.stack(
        [
            jnp.asarray(v, jnp.int32)
            for v in (space_at % 2, dp_at, space_at, space - 1, groups)
        ]
    )
    as_row = lambda v: v.reshape(1, -1)
    image = fields.reshape(rows, cols, chans)
    small = (as_row(expand_bias), dw_kernel, as_row(dw_bias))
    gain, bias = as_row(ln_gain), as_row(ln_bias)

    over_dp = lambda w: lax.ppermute(w, "dp", [(0, 1), (1, 0)])
    over_core = lambda w: lax.ppermute(w, "space", [(i, i ^ 1) for i in range(space)])
    later = info
    if pairs:
        shape = (chans, w_expand.shape[1] // 2)
        mine = share_weights(expand_share_kernel, info, [w_expand], [shape], "expand_share")
        expand_got = over_dp(mine[0])
        shapes = [
            (w_project.shape[0] // 2, w_project.shape[1]),
            (chans // 2, w_qkv.shape[1] + w_out.shape[1]),
        ]
        mine = share_weights(
            shares_kernel, after(info, *mine), [w_project, w_qkv, w_out], shapes, "other_shares"
        )
        project_got, rest_got = map(over_dp, mine)
        later = after(info, *mine)
    top, bottom = edge_rows(later, image)
    above = lax.ppermute(bottom, "space", [(i, (i + 1) % space) for i in range(space)])
    below = lax.ppermute(top, "space", [((i + 1) % space, i) for i in range(space)])
    sources = (image, above, below, as_row(bn_scale), as_row(bn_shift))
    if pairs:
        tiles = max(1, w_expand.shape[1] // 256)
        half = tiles // 2
        own_place = lambda i, t: i[DP] * tiles + t
        got_place = lambda i, t: (1 - i[DP]) * tiles + i[CORE] * half + t
        other_place = lambda i, t: (1 - i[DP]) * tiles + (1 - i[CORE]) * half + t
        own, ordered, normed = expand_some(info, sources, w_expand, *small, own_place, True)
        expand_got = after(expand_got, own)
        expand_other = over_core(expand_got)
        (got,) = expand_some(info, (normed,), expand_got, *small, got_place, False)
        expand_other, normed = lax.optimization_barrier((expand_other, normed, got))[:2]
        (other,) = expand_some(info, (normed,), expand_other, *small, other_place, False)
        spatial = [own, got, other]
        project_got = after(project_got, own)
        project_all = [w_project, project_got, over_core(project_got)]
    else:
        gathered = lambda w: lax.all_gather(w, "dp", axis=1, tiled=True)
        spatial, ordered, _ = expand_some(
            info, sources, gathered(w_expand), *small, lambda i, t: t, True
        )
        spatial = [spatial]
        project_all = [gathered(w_project)]
        w_qkv, w_out = gathered(w_qkv), gathered(w_out)


    def exchange(parts):
        parts = list(parts)
        for n in range(1, GRID):
            swap = [
                (s, (((s // groups) ^ MOVES[n]) * groups) + s % groups) for s in range(space)
            ]
            parts[n] = lax.ppermute(parts[n], "space", swap)
        return parts

    placed = project_rows(info, spatial, ordered, project_all, 0, rows, True)
    rest = []
    if pairs:
        rest_got = after(rest_got, placed[0])
        rest = [rest_got, over_core(rest_got)]
    back = exchange(attend(info, exchange(placed), gain, bias, w_qkv, w_out, rest))
    result = restore_rows(info, back, rows, 0, None)
    return result.reshape(fields.shape)


def solution(mesh):
    in_specs = (
        P("dp", "space", None, None),
        P(),
        P(),
        P(None, "dp"),
        P(),
        P(),
        P(),
        P(None, "dp"),
        P(),
        P(),
        P(None, "dp"),
        P(None, "dp"),
    )
    out_specs = P("dp", "space", None, None)
    return jax.shard_map(local, mesh=mesh, in_specs=in_specs, out_specs=out_specs, check_vma=False)
```

```python
import functools
import math

import jax
import jax.numpy as jnp
from jax import lax
from jax.experimental import pallas as pl
from jax.experimental.pallas import tpu as pltpu
from jax.sharding import PartitionSpec as P

HD = 32
GRID = 8
BATCH = 2
STRIPS = 2
MOVES = (0, 1, 4, 2, 6, 5, 7, 3)
ROOT = math.sqrt(2.0 / math.pi)
LIN = 2.0 * ROOT
CUBE = 8.0 * ROOT * 0.044715
F32 = jnp.float32
BF16 = jnp.bfloat16
VMEM_LIMIT = 18 * 1024 * 1024


def half_gelu(half):
    return half + half * jnp.tanh(half * (LIN + CUBE * (half * half)))


def one_hot_order(cols, inverse=False):
    stride = cols // GRID
    row = lax.broadcasted_iota(jnp.int32, (cols, cols), 0)
    col = lax.broadcasted_iota(jnp.int32, (cols, cols), 1)
    if inverse:
        row, col = col, row
    return jnp.where(col == (row % GRID) * stride + row // GRID, 1.0, 0.0).astype(BF16)


def dot(a, b):
    return jnp.dot(a, b, preferred_element_type=F32)


def vmem():
    return pl.BlockSpec(memory_space=pltpu.VMEM)


def smem():
    return pl.BlockSpec(memory_space=pltpu.SMEM)


def hbm():
    return pl.BlockSpec(memory_space=pltpu.HBM)


def in_hbm(array):
    return pltpu.with_memory_space_constraint(array, pltpu.HBM)


def any_space():
    return pl.BlockSpec(memory_space=pl.ANY)


def params():
    return pltpu.CompilerParams(vmem_limit_bytes=VMEM_LIMIT)


CORE, DP, SPACE, LAST, GROUPS = range(5)


def grid_of(info):
    return info[SPACE] // info[GROUPS]


def cost():
    return pl.CostEstimate(flops=1, bytes_accessed=1, transcendentals=1)


def copy_all(pairs, sems):
    copies = [pltpu.make_async_copy(src, dst, sems.at[n]) for n, (src, dst) in enumerate(pairs)]
    for copy in copies:
        copy.start()
    return copies


def edges_kernel(info, image, top, bottom, sems):
    rows = image.shape[0]
    for copy in copy_all([(image.at[rows - 1 : rows], bottom), (image.at[0:1], top)], sems):
        copy.wait()


def edge_rows(info, image):
    edge = jax.ShapeDtypeStruct((1,) + image.shape[1:], BF16)
    return pl.pallas_call(
        edges_kernel,
        in_specs=[smem(), hbm()],
        out_specs=[vmem()] * 2,
        out_shape=[edge, edge],
        scratch_shapes=[pltpu.SemaphoreType.DMA((2,))],
        compiler_params=params(),
        name="edge_rows",
    )(info, in_hbm(image))


def shares_kernel(info, expand, project, qkv, out, expand_part, project_part, rest_part, sems):
    def span(part, axis):
        size = part.shape[axis]
        return pl.ds(pl.multiple_of(info[CORE] * size, size), size)

    width = qkv.shape[1]
    moves = [
        (expand.at[:, span(expand_part, 1)], expand_part),
        (project.at[span(project_part, 0)], project_part),
        (qkv.at[span(rest_part, 0)], rest_part.at[:, :width]),
        (out.at[span(rest_part, 0)], rest_part.at[:, width:]),
    ]
    for copy in copy_all(moves, sems):
        copy.wait()


def share_weights(info, w_expand, w_project, w_qkv, w_out):
    shapes = [
        (w_expand.shape[0], w_expand.shape[1] // 2),
        (w_project.shape[0] // 2, w_project.shape[1]),
        (w_qkv.shape[0] // 2, w_qkv.shape[1] + w_out.shape[1]),
    ]
    return pl.pallas_call(
        shares_kernel,
        in_specs=[smem()] + [hbm()] * 4,
        out_specs=[vmem()] * 3,
        out_shape=[jax.ShapeDtypeStruct(shape, BF16) for shape in shapes],
        scratch_shapes=[pltpu.SemaphoreType.DMA((4,))],
        compiler_params=params(),
        name="share_weights",
    )(info, *map(in_hbm, (w_expand, w_project, w_qkv, w_out)))


def order_kernel(image, above, below, scale, shift, ordered, normed):
    rows, cols, _ = image.shape
    pick = one_hot_order(cols)
    for row in range(rows + 2):
        if row == 0:
            placed = dot(pick, above[0])
        elif row == rows + 1:
            placed = dot(pick, below[0])
        else:
            placed = dot(pick, image[row - 1])
            ordered[row - 1] = placed.astype(BF16)
        normed[row] = (
            placed * (0.5 * scale[...]) + 0.5 * shift[...]
        ).astype(BF16)


def expand_kernel(first, tile_of, info, *refs):
    refs = list(refs)
    take = lambda n: [refs.pop(0) for _ in range(n)]
    step = pl.program_id(0)
    if first:
        image, above, below, scale, shift, weight, bias, taps, tap_bias = take(9)
        out, ordered, normed = take(3)
        raw, wide, sems, *held = refs
        moved = [(image, held[0])]
        moved += list(zip((scale, shift, weight, bias, taps, tap_bias), held[1:]))
        image, scale, shift, weight, bias, taps, tap_bias = held

        @pl.when(step == 0)
        def _():
            copies = copy_all(moved, sems)
            for copy in copies:
                copy.wait()
            order_kernel(image, above, below, scale, shift, ordered, normed)

    else:
        normed, weight, bias, taps, tap_bias, out, raw, wide = refs
    width = raw.shape[1]
    cols = wide.shape[1] - 2 * GRID
    rows = wide.shape[0] - 2
    if first:
        here = pl.ds(pl.multiple_of(step * width, width), width)
        tile = pl.ds(pl.multiple_of(tile_of(info, step) * width, width), width)
    else:
        here = tile = slice(None)
    weight = weight[:, here]
    half_bias = 0.5 * bias[:, tile]
    half_taps = 0.5 * taps[:, :, tile]
    half_tap_bias = 0.5 * tap_bias[:, tile]
    lane = lax.broadcasted_iota(jnp.int32, (GRID, width), 0)
    strip = cols // STRIPS
    blocks = [slice(lane, lane + 128) for lane in range(0, width, 128)]

    def product(row):
        tokens = normed[row : row + BATCH].reshape(BATCH * cols, -1)
        raw[row * cols : (row + BATCH) * cols, :] = dot(tokens, weight)

    def activate(row):
        value = half_gelu(raw[row * cols : (row + 1) * cols, :] + half_bias)
        if row == 0:
            value = value * jnp.where(info[SPACE] > 0, 1.0, 0.0)
        elif row == rows + 1:
            value = value * jnp.where(info[SPACE] < info[LAST], 1.0, 0.0)
        wide[row, GRID : GRID + cols, :] = value
        head = value[:GRID]
        tail = value[cols - GRID :]
        wide[row, :GRID, :] = jnp.where(lane == 0, 0.0, pltpu.roll(tail, 1, 0))
        wide[row, GRID + cols :, :] = jnp.where(
            lane == GRID - 1, 0.0, pltpu.roll(head, GRID - 1, 0)
        )

    def convolve(row):
        for lanes in blocks:
            for start in range(0, cols, strip):
                near = [
                    wide[row + off, start : start + strip + 2 * GRID, lanes] for off in range(3)
                ]
                total = half_tap_bias[:, lanes]
                for col_off in range(3):
                    for row_off in range(3):
                        part = near[row_off][GRID * col_off : GRID * col_off + strip]
                        total = total + part * half_taps[row_off, col_off, lanes][None]
                at = row * cols + start
                out[at : at + strip, lanes] = half_gelu(total).astype(BF16)

    product(0)
    for first_row in range(0, rows + 2, BATCH):
        if first_row + BATCH < rows + 2:
            product(first_row + BATCH)
        for row in range(first_row, first_row + BATCH):
            activate(row)
            if row >= 2:
                convolve(row - 2)


def expand_some(info, sources, weight, bias, taps, tap_bias, tile_of, first):
    chans, here = weight.shape
    width = min(256, here)
    if first:
        rows, cols, _ = sources[0].shape
    else:
        rows, cols = sources[0].shape[0] - 2, sources[0].shape[1]
    whole = lambda shape: pl.BlockSpec(shape, lambda t, info: (0,) * len(shape))
    held = []
    if first:
        in_specs = [hbm(), whole(sources[1].shape), whole(sources[2].shape)] + [hbm()] * 6
        fetched = [sources[0], *sources[3:], weight, bias, taps, tap_bias]
        held = [pltpu.SemaphoreType.DMA((len(fetched),))]
        held += [pltpu.VMEM(f.shape, f.dtype) for f in fetched]
    else:
        in_specs = [whole(s.shape) for s in sources]
        in_specs += [
            pl.BlockSpec((chans, width), lambda t, info: (0, t)),
            pl.BlockSpec((1, width), lambda t, info: (0, tile_of(info, t))),
            pl.BlockSpec((3, 3, width), lambda t, info: (0, 0, tile_of(info, t))),
            pl.BlockSpec((1, width), lambda t, info: (0, tile_of(info, t))),
        ]
    operands = [info, *sources, weight, bias, taps, tap_bias]
    if first:
        operands = [o if n in (0, 2, 3) else in_hbm(o) for n, o in enumerate(operands)]
    out_specs = [pl.BlockSpec((rows * cols, width), lambda t, info: (0, t))]
    out_shape = [jax.ShapeDtypeStruct((rows * cols, here), BF16)]
    if first:
        shapes = [(rows, cols, chans), (rows + 2, cols, chans)]
        out_specs += [whole(shape) for shape in shapes]
        out_shape += [jax.ShapeDtypeStruct(shape, BF16) for shape in shapes]
    return pl.pallas_call(
        functools.partial(expand_kernel, first, tile_of),
        grid_spec=pltpu.PrefetchScalarGridSpec(
            num_scalar_prefetch=1,
            grid=(here // width,),
            in_specs=in_specs,
            out_specs=out_specs,
            scratch_shapes=[
                pltpu.VMEM(((rows + 2) * cols, width), F32),
                pltpu.VMEM((rows + 2, cols + 2 * GRID, width), F32),
                *held,
            ],
        ),
        out_shape=out_shape,
        compiler_params=params(),
        cost_estimate=cost(),
        name="expand_conv",
    )(*operands)


def pieced_dot(lhs, pieces, info, put):
    width = pieces[0].shape[1]
    if len(pieces) == 1:
        put(0, width, dot(lhs[...], pieces[0][...]))
        return
    put(pl.multiple_of(info[DP] * width, width), width, dot(lhs[...], pieces[0][...]))
    total = None
    for n, piece in enumerate(pieces[1:]):
        depth = piece.shape[0]
        at = 1 - info[CORE] if n else info[CORE]
        part = dot(lhs[:, pl.ds(pl.multiple_of(at * depth, depth), depth)], piece[...])
        total = part if total is None else total + part
    put(pl.multiple_of((1 - info[DP]) * width, width), width, total)


def project_kernel(pieces, split, info, ordered, *refs):
    refs = list(refs)
    take = lambda n: [refs.pop(0) for _ in range(n)]
    spatial, weights, outs, (conv, other) = take(pieces), take(pieces), take(GRID if split else 1), refs
    count, cols, chans = ordered.shape
    size = cols // GRID
    own = weights[0]
    width = own.shape[1]

    def put(start, product):
        span = pl.ds(start, width)
        for row in range(count):
            at = slice(row * cols, (row + 1) * cols)
            conv[at, span] = (ordered[row, :, span].astype(F32) + product[at]).astype(BF16)

    if pieces == 1:
        put(0, dot(spatial[0][...], own[...]))
    else:
        mine, core = info[DP], info[CORE]
        half = own.shape[0] // 2
        for n, at in ((1, core), (2, 1 - core)):
            other[pl.ds(pl.multiple_of(at * half, half), half), :] = weights[n][...]
        part = half // 2
        starts = (
            (mine * half, half),
            ((1 - mine) * half + core * part, part),
            ((1 - mine) * half + (1 - core) * part, part),
        )
        for weight, column in ((own, mine), (other, 1 - mine)):
            total = None
            for lhs, (start, depth) in zip(spatial, starts):
                rows = pl.ds(pl.multiple_of(start, part), depth)
                product = dot(lhs[...], weight[rows, :])
                total = product if total is None else total + product
            put(pl.multiple_of(column * width, width), total)

    for k in range(GRID):
        place = (grid_of(info) ^ MOVES[k]) if split else k
        for row in range(count):
            start = row * cols + pl.multiple_of(place * size, size)
            block_of(outs, k)[row] = conv[pl.ds(start, size), :]


def block_of(parts, k):
    return parts[k] if len(parts) > 1 else parts[0].at[k]


def project_rows(info, spatial, ordered, weights, chunk, count, split):
    rows, cols, chans = ordered.shape
    size = cols // GRID
    block = (count, size, chans)
    outs = [block] * GRID if split else [(GRID,) + block]
    whole = lambda shape: pl.BlockSpec(shape, lambda t, info: (0,) * len(shape))
    return pl.pallas_call(
        functools.partial(project_kernel, len(weights), split),
        grid_spec=pltpu.PrefetchScalarGridSpec(
            num_scalar_prefetch=1,
            grid=(1,),
            in_specs=[pl.BlockSpec((count, cols, chans), lambda t, info: (chunk, 0, 0))]
            + [pl.BlockSpec((count * cols, s.shape[1]), lambda t, info: (chunk, 0)) for s in spatial]
            + [whole(w.shape) for w in weights],
            out_specs=[whole(out) for out in outs],
            scratch_shapes=[pltpu.VMEM((count * cols, chans), BF16), pltpu.VMEM(weights[0].shape, BF16)],
        ),
        out_shape=[jax.ShapeDtypeStruct(out, BF16) for out in outs],
        compiler_params=params(),
        cost_estimate=cost(),
        name="project_rows",
    )(info, ordered, *spatial, *weights)


def attend_kernel(pieces, blocks, info, gain, bias, *refs):
    refs = list(refs)
    take = lambda n: [refs.pop(0) for _ in range(n)]
    qkv_pieces, out_pieces, rest = take(1), take(1), take(pieces - 1)
    split = qkv_pieces[0].shape[1]
    for both in rest:
        qkv_pieces.append(both.at[:, :split])
        out_pieces.append(both.at[:, split:])
    tokens, outs = take(blocks), take(blocks)
    lned, triple, mixed, resid, soft = refs
    count, size, chans = tokens[0].shape[-3:]
    wins = size // GRID
    length = GRID * GRID
    group = min(128, chans)
    heads = group // HD
    keys = heads * length

    for a in range(count):
        rows = [block_of(tokens, k)[a].astype(F32) for k in range(GRID)]
        for w in range(wins):
            x = jnp.concatenate([r[w * GRID : (w + 1) * GRID] for r in rows], axis=0)
            start = (a * wins + w) * length
            resid[start : start + length, :] = x
            center = jnp.mean(x, axis=-1, keepdims=True)
            off = x - center
            spread = jnp.mean(off * off, axis=-1, keepdims=True)
            lned[start : start + length, :] = (
                off * lax.rsqrt(spread + 1e-05) * gain[...] + bias[...]
            ).astype(BF16)

    def put_triple(start, width, product):
        triple[:, pl.ds(start, width)] = product.astype(BF16)

    pieced_dot(lned, qkv_pieces, info, put_triple)

    def same(shape, row_block, col_block):
        row = lax.broadcasted_iota(jnp.int32, shape, 0) // row_block
        col = lax.broadcasted_iota(jnp.int32, shape, 1) // col_block
        return jnp.where(row == col, 1.0, 0.0).astype(BF16)

    spread_mask = same((keys, group), length, HD)
    sum_mask = same((256, 256), length, length)
    factor = math.log2(math.e) / math.sqrt(HD)
    each = [(win, g) for win in range(count * wins) for g in range(chans // group)]
    spot = lambda win, g: (
        slice(win * length, (win + 1) * length),
        slice(g * keys, (g + 1) * keys),
    )
    for win, g in each:
        at, lanes = spot(win, g)
        query = triple[at, g * group : (g + 1) * group]
        key = triple[at, chans + g * group : chans + (g + 1) * group]
        key_wide = jnp.concatenate([key] * heads, axis=0) * spread_mask
        scores = lax.dot_general(
            query, key_wide, (((1,), (1,)), ((), ())), preferred_element_type=F32
        )
        soft[at, lanes] = jnp.minimum(jnp.exp2(scores * factor), 3.3895e38).astype(BF16)
    for start in range(0, count * wins * length, 256):
        for lane in range(0, soft.shape[1], 256):
            at, lanes = slice(start, start + 256), slice(lane, lane + 256)
            exponent = soft[at, lanes]
            soft[at, lanes] = (exponent.astype(F32) / dot(exponent, sum_mask)).astype(BF16)
    for win, g in each:
        at, lanes = spot(win, g)
        value = triple[at, 2 * chans + g * group : 2 * chans + (g + 1) * group]
        value_wide = jnp.concatenate([value] * heads, axis=0) * spread_mask
        mixed[at, g * group : (g + 1) * group] = dot(soft[at, lanes], value_wide).astype(BF16)

    def put_out(start, width, product):
        span = pl.ds(start, width)
        resid[:, span] = resid[:, span] + product

    pieced_dot(mixed, out_pieces, info, put_out)
    for a in range(count):
        for k in range(GRID):
            parts = []
            for w in range(wins):
                start = (a * wins + w) * length + k * GRID
                parts.append(resid[start : start + GRID, :])
            block_of(outs, k)[a] = jnp.concatenate(parts, axis=0).astype(BF16)


def attend(info, tokens, gain, bias, w_qkv, w_out, rest):
    count, size, chans = tokens[0].shape[-3:]
    total = count * size * GRID
    return pl.pallas_call(
        functools.partial(attend_kernel, 1 + len(rest), len(tokens)),
        out_shape=[jax.ShapeDtypeStruct(t.shape, BF16) for t in tokens],
        in_specs=[smem()] + [vmem()] * (4 + len(rest) + len(tokens)),
        out_specs=[vmem()] * len(tokens),
        scratch_shapes=[
            pltpu.VMEM((total, chans), BF16),
            pltpu.VMEM((total, 3 * chans), BF16),
            pltpu.VMEM((total, chans), BF16),
            pltpu.VMEM((total, chans), F32),
            pltpu.VMEM((total, chans // HD * GRID * GRID), BF16),
        ],
        compiler_params=params(),
        cost_estimate=cost(),
        name="attend",
    )(info, gain, bias, w_qkv, w_out, *rest, *tokens)


def restore_kernel(blocks, info, *refs):
    parts = refs[:blocks]
    out, buf = refs[-2:]
    count, cols, chans = out.shape
    size = cols // GRID
    back = one_hot_order(cols, inverse=True)
    for row in range(count):
        if blocks == 1:
            tokens = parts[0][:, row].reshape(cols, chans)
        else:
            for k in range(GRID):
                place = pl.multiple_of((grid_of(info) ^ MOVES[k]) * size, size)
                buf[pl.ds(row * cols + place, size), :] = parts[k][row]
            tokens = buf[row * cols : (row + 1) * cols, :]
        out[row] = dot(back, tokens).astype(BF16)


def restore_rows(info, parts, rows, chunk, out):
    count, size, chans = parts[0].shape[-3:]
    cols = size * GRID
    in_specs = [pl.BlockSpec(p.shape, lambda t, i, n=p.ndim: (0,) * n) for p in parts]
    operands = [info, *parts]
    aliases = {}
    if out is not None:
        in_specs.append(pl.BlockSpec(memory_space=pl.ANY))
        aliases = {len(operands): 0}
        operands.append(out)
    return pl.pallas_call(
        functools.partial(restore_kernel, len(parts)),
        grid_spec=pltpu.PrefetchScalarGridSpec(
            num_scalar_prefetch=1,
            grid=(1,),
            in_specs=in_specs,
            out_specs=pl.BlockSpec((count, cols, chans), lambda t, info: (chunk, 0, 0)),
            scratch_shapes=[pltpu.VMEM((count * cols, chans), BF16)],
        ),
        out_shape=jax.ShapeDtypeStruct((rows, cols, chans), BF16),
        input_output_aliases=aliases,
        compiler_params=params(),
        cost_estimate=cost(),
        name="restore_rows",
    )(*operands)


def after(value, *others):
    return lax.optimization_barrier((value, *others))[0]


def local(
    fields,
    bn_scale,
    bn_shift,
    w_expand,
    expand_bias,
    dw_kernel,
    dw_bias,
    w_project,
    ln_gain,
    ln_bias,
    w_qkv,
    w_out,
):
    _, rows, cols, chans = fields.shape
    dp, space = lax.axis_size("dp"), lax.axis_size("space")
    dp_at, space_at = lax.axis_index("dp"), lax.axis_index("space")
    groups = space // GRID
    pairs = dp == 2 and space % 2 == 0
    info = jnp.stack(
        [
            jnp.asarray(v, jnp.int32)
            for v in (space_at % 2, dp_at, space_at, space - 1, groups)
        ]
    )
    as_row = lambda v: v.reshape(1, -1)
    image = fields.reshape(rows, cols, chans)
    small = (as_row(expand_bias), dw_kernel, as_row(dw_bias))
    gain, bias = as_row(ln_gain), as_row(ln_bias)

    over_dp = lambda w: lax.ppermute(w, "dp", [(0, 1), (1, 0)])
    over_core = lambda w: lax.ppermute(w, "space", [(i, i ^ 1) for i in range(space)])
    later = info
    if pairs:
        mine = share_weights(info, w_expand, w_project, w_qkv, w_out)
        expand_got, project_got, rest_got = map(over_dp, mine)
        later = after(info, *mine)
    top, bottom = edge_rows(later, image)
    above = lax.ppermute(bottom, "space", [(i, (i + 1) % space) for i in range(space)])
    below = lax.ppermute(top, "space", [((i + 1) % space, i) for i in range(space)])
    sources = (image, above, below, as_row(bn_scale), as_row(bn_shift))
    if pairs:
        tiles = max(1, w_expand.shape[1] // 256)
        half = tiles // 2
        own_place = lambda i, t: i[DP] * tiles + t
        got_place = lambda i, t: (1 - i[DP]) * tiles + i[CORE] * half + t
        other_place = lambda i, t: (1 - i[DP]) * tiles + (1 - i[CORE]) * half + t
        own, ordered, normed = expand_some(info, sources, w_expand, *small, own_place, True)
        expand_got = after(expand_got, own)
        expand_other = over_core(expand_got)
        (got,) = expand_some(info, (normed,), expand_got, *small, got_place, False)
        expand_other, normed = lax.optimization_barrier((expand_other, normed, got))[:2]
        (other,) = expand_some(info, (normed,), expand_other, *small, other_place, False)
        spatial = [own, got, other]
        project_got = after(project_got, own)
        project_all = [w_project, project_got, over_core(project_got)]
    else:
        gathered = lambda w: lax.all_gather(w, "dp", axis=1, tiled=True)
        spatial, ordered, _ = expand_some(
            info, sources, gathered(w_expand), *small, lambda i, t: t, True
        )
        spatial = [spatial]
        project_all = [gathered(w_project)]
        w_qkv, w_out = gathered(w_qkv), gathered(w_out)


    def exchange(parts):
        parts = list(parts)
        for n in range(1, GRID):
            swap = [
                (s, (((s // groups) ^ MOVES[n]) * groups) + s % groups) for s in range(space)
            ]
            parts[n] = lax.ppermute(parts[n], "space", swap)
        return parts

    placed = project_rows(info, spatial, ordered, project_all, 0, rows, True)
    rest = []
    if pairs:
        rest_got = after(rest_got, placed[0])
        rest = [rest_got, over_core(rest_got)]
    back = exchange(attend(info, exchange(placed), gain, bias, w_qkv, w_out, rest))
    result = restore_rows(info, back, rows, 0, None)
    return result.reshape(fields.shape)


def solution(mesh):
    in_specs = (
        P("dp", "space", None, None),
        P(),
        P(),
        P(None, "dp"),
        P(),
        P(),
        P(),
        P(None, "dp"),
        P(),
        P(),
        P(None, "dp"),
        P(None, "dp"),
    )
    out_specs = P("dp", "space", None, None)
    return jax.shard_map(local, mesh=mesh, in_specs=in_specs, out_specs=out_specs, check_vma=False)
```
